1024 devices in a mesh: expert: 32 (over z), mp: 32 (over y, x, core).
Axes of the slice: x: 4, y: 4, z: 32, core: 2. Of those that a mesh axis runs over, the one named last changes fastest.
Arguments:
- x_tokens: bfloat16 [4096, 2048], P('expert', 'mp'), may hold values from -6 to 6
- cotangent: bfloat16 [4096, 2048], P('expert', 'mp'), may hold values from -2 to 2
- w_gate: bfloat16 [32, 1024, 8192], P('expert', None, 'mp'), may hold values from -0.125 to 0.125
- w_up: bfloat16 [32, 1024, 8192], P('expert', None, 'mp'), may hold values from -0.125 to 0.125
- w_down: bfloat16 [32, 8192, 1024], P('expert', 'mp'), may hold values from -0.125 to 0.125
- combine: float32 [64, 128], P('expert'), may hold values from 0.1 to 1
- indices: int32 [64, 128], replicated, may hold values from -1 to 4095, as said below
Outputs:
- grad_tokens: bfloat16 [4096, 2048], P('expert', 'mp')
- grad_gate: bfloat16 [32, 1024, 8192], P('expert', None, 'mp')
- grad_up: bfloat16 [32, 1024, 8192], P('expert', None, 'mp')
- grad_down: bfloat16 [32, 8192, 1024], P('expert', 'mp')
- grad_combine: float32 [64, 128], P('expert')
The draws below stay inside these ranges and needn't reach their ends.
Inputs may be any that keep to these rules, and one draw needn't show every extreme that they name: `indices`: each row lists the tokens one expert chose, in increasing order, then -1 in its remaining slots. Tokens are owned in blocks of 128 along expert; one expert takes at most 8 tokens from one block, and in every row some block gives exactly 8. In every draw some expert fills all 128 slots.
All inputs are finite; a program needn't handle non-finite values.
Results may differ from the reference program's by a relative error of at most 0.022.
Values may be sent and summed in bfloat16 or wider, within the bound.
No kernel may reach another device: no remote copies, remote signals or barrier semaphores. Data moves between devices by JAX's collectives and lax.ppermute only.
A program may use at most 32 MiB of HBM per device.

```python
import jax
import jax.numpy as jnp
from jax import lax

D = 2048
FF = 2048
EXP_DEV = 2
TOK_DEV = 128
GROUPS = 32
EXPERTS = 64
TOKENS = 4096
CAP = 128
PEER = 8
N_EXPERT = 32
N_MP = 32


def draw_indices(key, part):
    key = jax.random.fold_in(key, 7)
    keys = jax.random.split(key, 6)
    pairs = N_EXPERT // 2
    first_count = jax.random.randint(keys[0], (EXPERTS, pairs), PEER // 4, PEER + 1)
    remaining = PEER - first_count
    second_count = jax.random.randint(keys[1], (EXPERTS, pairs), remaining // 2, remaining + 1)
    forced_pair = jax.random.randint(keys[2], (EXPERTS, 1), 0, pairs)
    pair_ids = jnp.arange(pairs, dtype=jnp.int32)[None, :]
    first_count = jnp.where(pair_ids == forced_pair, PEER, first_count)
    full_expert = jax.random.randint(keys[3], (), 0, EXPERTS)
    expert_ids = jnp.arange(EXPERTS, dtype=jnp.int32)[:, None]
    second_count = jnp.where(expert_ids == full_expert, PEER - first_count, second_count)
    second_count = jnp.where(pair_ids == forced_pair, 0, second_count)
    paired = jnp.concatenate([first_count, second_count], axis=1)
    orders = jax.vmap(lambda item: jax.random.permutation(item, N_EXPERT))(jax.random.split(keys[4], EXPERTS))
    counts = jnp.take_along_axis(paired, orders, axis=1)
    ranks = jax.vmap(lambda item: jax.random.permutation(item, TOK_DEV))(jax.random.split(keys[5], EXPERTS * N_EXPERT))
    ranks = ranks.reshape(EXPERTS, N_EXPERT, TOK_DEV)
    picked = (ranks < counts[:, :, None]).reshape(EXPERTS, TOKENS)
    position = jnp.cumsum(picked.astype(jnp.int32), axis=1) - 1
    position = jnp.where(picked, position, CAP)
    token_ids = jnp.broadcast_to(jnp.arange(TOKENS, dtype=jnp.int32)[None, :], (EXPERTS, TOKENS))
    row_ids = jnp.broadcast_to(jnp.arange(EXPERTS, dtype=jnp.int32)[:, None], (EXPERTS, TOKENS))
    table = jnp.full((EXPERTS, CAP + 1), -1, jnp.int32).at[row_ids, position].set(token_ids)
    return table[:, :CAP]


def steps_of(own_key, extent, cuts, least, top_value):
    loudness = 1.0
    for dim, blocks in cuts:
        draws = jax.random.uniform(jax.random.fold_in(jax.random.fold_in(own_key, 6), dim), (blocks,), jnp.float32, least / len(cuts), top_value / len(cuts))
        loudness = loudness * jnp.repeat(jnp.exp(draws), extent[dim] // blocks).reshape((-1,) + (1,) * (len(extent) - 1 - dim))
    return loudness


def noise(own_key, extent, scale, bound, cuts=(), kind=jnp.bfloat16):
    entries = scale * jax.random.normal(own_key, extent, jnp.float32)
    if cuts:
        entries = entries * steps_of(own_key, extent, cuts, -0.22, 0.18)
    return jnp.clip(entries, -bound, bound).astype(kind)


def setup_inputs(seed: int = 0) -> dict:
    arg_keys = jax.random.split(jax.random.key(seed), 8)
    return {
        "x_tokens": noise(arg_keys[0], (TOKENS, D), 1.0, 6.0, ((0, 32), (1, 32))),
        "cotangent": noise(arg_keys[1], (TOKENS, D), 0.3, 2.0, ((0, 32), (1, 32))),
        "w_gate": noise(arg_keys[2], (GROUPS, D // 2, 2 * EXP_DEV * FF), D ** -0.5, 0.125, ((0, 32), (2, 32))),
        "w_up": noise(arg_keys[3], (GROUPS, D // 2, 2 * EXP_DEV * FF), D ** -0.5, 0.125, ((0, 32), (2, 32))),
        "w_down": noise(arg_keys[4], (GROUPS, 2 * EXP_DEV * FF, D // 2), FF ** -0.5, 0.125, ((0, 32), (1, 32))),
        "combine": jnp.clip(0.1 + 0.9 * jax.random.uniform(arg_keys[5], (EXPERTS, CAP), jnp.float32) ** steps_of(arg_keys[5], (EXPERTS, CAP), ((0, 32),), -0.2, 0.2), 0.1, 1.0),
        "indices": draw_indices(jax.random.fold_in(arg_keys[7], 71), 0),
    }


def expert_grads(rows_in, rows_out, wg, wu, wd, slot_weight):
    gate_pre = jnp.dot(rows_in, wg, preferred_element_type=jnp.float32)
    up_pre = jnp.dot(rows_in, wu, preferred_element_type=jnp.float32)
    sigmoid_gate = jax.nn.sigmoid(gate_pre)
    activation = (gate_pre * sigmoid_gate * up_pre).astype(jnp.bfloat16)
    back_grad = lax.dot_general(rows_out, wd, (((1,), (1,)), ((), ())), preferred_element_type=jnp.float32)
    slot_term = jnp.sum(activation.astype(jnp.float32) * back_grad, axis=1)
    scaled_out = (slot_weight[:, None] * rows_out.astype(jnp.float32)).astype(jnp.bfloat16)
    grad_down = lax.dot_general(activation, scaled_out, (((0,), (0,)), ((), ())), preferred_element_type=jnp.float32).astype(jnp.bfloat16)
    d_act = slot_weight[:, None] * back_grad
    d_gate = (d_act * up_pre * sigmoid_gate * (1.0 + gate_pre * (1.0 - sigmoid_gate))).astype(jnp.bfloat16)
    d_up = (d_act * gate_pre * sigmoid_gate).astype(jnp.bfloat16)
    grad_gate = lax.dot_general(rows_in, d_gate, (((0,), (0,)), ((), ())), preferred_element_type=jnp.float32).astype(jnp.bfloat16)
    grad_up = lax.dot_general(rows_in, d_up, (((0,), (0,)), ((), ())), preferred_element_type=jnp.float32).astype(jnp.bfloat16)
    blocks = N_MP // (2 * EXP_DEV)
    block_width = FF // blocks
    pieces = jnp.einsum("cbh,dbh->bcd", d_gate.astype(jnp.float32).reshape(CAP, blocks, block_width),
                        wg.astype(jnp.float32).reshape(D, blocks, block_width), precision=lax.Precision.HIGHEST)
    pieces = pieces + jnp.einsum("cbh,dbh->bcd", d_up.astype(jnp.float32).reshape(CAP, blocks, block_width),
                                 wu.astype(jnp.float32).reshape(D, blocks, block_width), precision=lax.Precision.HIGHEST)
    rounded = lax.optimization_barrier(pieces.astype(jnp.bfloat16))
    contrib = jnp.sum(rounded.astype(jnp.float32), axis=0)
    return slot_term, grad_gate, grad_up, grad_down, contrib


def unpack_in(group_weight, member):
    part = group_weight.reshape(D // 2, EXP_DEV, 2, FF)[:, member]
    return jnp.transpose(part, (1, 0, 2)).reshape(D, FF)


def pack_in(mats):
    stacked = jnp.stack(mats).reshape(EXP_DEV, 2, D // 2, FF)
    return jnp.transpose(stacked, (2, 0, 1, 3)).reshape(D // 2, 2 * EXP_DEV * FF)


def unpack_down(group_weight, member):
    part = group_weight.reshape(EXP_DEV, 2, FF, D // 2)[member]
    return jnp.transpose(part, (1, 0, 2)).reshape(FF, D)


def pack_down(mats):
    stacked = jnp.stack(mats).reshape(EXP_DEV, FF, 2, D // 2)
    return jnp.transpose(stacked, (0, 2, 1, 3)).reshape(2 * EXP_DEV * FF, D // 2)


def reference(x_tokens, cotangent, w_gate, w_up, w_down, combine, indices):
    def one_group(group_index):
        wg_group = lax.dynamic_index_in_dim(w_gate, group_index, 0, keepdims=False)
        wu_group = lax.dynamic_index_in_dim(w_up, group_index, 0, keepdims=False)
        wd_group = lax.dynamic_index_in_dim(w_down, group_index, 0, keepdims=False)
        terms, gates, ups, downs, contribs = [], [], [], [], []
        for member in range(EXP_DEV):
            expert_id = group_index * EXP_DEV + member
            chosen = lax.dynamic_index_in_dim(indices, expert_id, 0, keepdims=False)
            slot_weight = lax.dynamic_index_in_dim(combine, expert_id, 0, keepdims=False)
            slot_valid = chosen >= 0
            safe = jnp.where(slot_valid, chosen, 0).astype(jnp.int32)
            rows_in = jnp.where(slot_valid[:, None], x_tokens[safe], jnp.zeros((), jnp.bfloat16))
            rows_out = jnp.where(slot_valid[:, None], cotangent[safe], jnp.zeros((), jnp.bfloat16))
            wg = unpack_in(wg_group, member)
            wu = unpack_in(wu_group, member)
            wd = unpack_down(wd_group, member)
            result = expert_grads(rows_in, rows_out, wg, wu, wd, slot_weight)
            terms.append(result[0])
            gates.append(result[1])
            ups.append(result[2])
            downs.append(result[3])
            contribs.append(result[4])
        return (jnp.stack(terms), pack_in(gates), pack_in(ups), pack_down(downs), jnp.stack(contribs))

    terms, grad_gate, grad_up, grad_down, contribs = lax.map(one_group, jnp.arange(N_EXPERT, dtype=jnp.int32))
    grad_combine = terms.reshape(EXPERTS, CAP)
    targets = jnp.where(indices >= 0, indices, TOKENS).astype(jnp.int32).reshape(-1)
    summed = jnp.zeros((TOKENS + 1, D), jnp.float32).at[targets].add(contribs.reshape(-1, D))
    grad_tokens = summed[:TOKENS].astype(jnp.bfloat16)
    return grad_tokens, grad_gate, grad_up, grad_down, grad_combine
```

```python
import jax
import jax.numpy as jnp
from jax import lax
from jax.sharding import Mesh
from jax.sharding import PartitionSpec as P


def local(x_tokens, cotangent, w_gate, w_up, w_down, combine, indices):
    bf16 = jnp.bfloat16
    f32 = jnp.float32
    groups = lax.axis_size("z")
    spread = lax.axis_size("x") * lax.axis_size("c")
    tok_dev, part = x_tokens.shape
    experts, capacity = indices.shape
    exp_dev = experts // groups
    peer = 2 * capacity // groups
    z = lax.axis_index("z")
    p = lax.axis_index("p")
    q = lax.axis_index("q")
    wg = w_gate[0]
    wu = w_up[0]
    wd = w_down[0]

    table = jnp.concatenate([x_tokens, cotangent], axis=1)
    table = lax.ppermute(table, ("p", "q"), [(0, 0), (1, 2), (2, 1), (3, 3)])

    slots = jnp.arange(capacity, dtype=jnp.int32)
    places = jnp.arange(peer, dtype=jnp.int32)
    tokens = jnp.arange(tok_dev, dtype=jnp.int32)
    ordered = jnp.transpose(indices.reshape(groups, exp_dev, capacity), (1, 0, 2)).reshape(
        experts, capacity
    )
    base = z * tok_dev
    start = jnp.sum(((ordered >= 0) & (ordered < base)).astype(jnp.int32), axis=1)
    want = start[:, None] + places[None, :]
    shifted = jnp.where(ordered >= 0, ordered - base + 1, 0)
    chosen = (
        jnp.sum(jnp.where(slots[None, None, :] == want[:, :, None], shifted[:, None, :], 0), axis=2)
        - 1
    )
    pick = (chosen[:, :, None] == tokens[None, None, :]).astype(bf16)
    pick = pick.reshape(experts * peer, tok_dev)
    send = jnp.dot(pick, table, preferred_element_type=f32).astype(bf16)
    recv = lax.all_to_all(
        send.reshape(experts, peer, 2 * part), ("p", "z"), split_axis=0, concat_axis=0, tiled=True
    )

    own = lax.dynamic_index_in_dim(indices, z * exp_dev + p, 0, keepdims=False)
    blocks = jnp.arange(groups, dtype=jnp.int32)
    own_start = jnp.sum(
        ((own[None, :] >= 0) & (own[None, :] < blocks[:, None] * tok_dev)).astype(jnp.int32), axis=1
    )
    own_want = own_start[:, None] + places[None, :]
    own_block = jnp.where(own >= 0, own // tok_dev, -1)
    place = (slots[:, None, None] == own_want[None]) & (
        own_block[:, None, None] == blocks[None, :, None]
    )
    place = place.astype(bf16).reshape(capacity, groups * peer)
    recv = recv.reshape(2, groups * peer, 2 * part)
    compact = jnp.concatenate(
        [jnp.dot(place, recv[i], preferred_element_type=f32).astype(bf16) for i in range(2)], axis=1
    )
    gathered = lax.all_gather(compact, ("x", "c"), axis=0)
    gathered = gathered.reshape(spread, capacity, 2, 2, part)
    rows = jnp.transpose(gathered, (3, 1, 2, 0, 4)).reshape(2, capacity, 2 * spread * part)
    rows_in = rows[0]
    rows_out = rows[1]

    hidden = wg.shape[1]
    gate_mine = jnp.dot(rows_in, wg, preferred_element_type=f32)
    up_mine = jnp.dot(rows_in, wu, preferred_element_type=f32)
    back_mine = lax.dot_general(rows_out, wd, (((1,), (1,)), ((), ())), preferred_element_type=f32)
    mine = jnp.concatenate([gate_mine, up_mine, back_mine], axis=1)
    other = lax.ppermute(mine.astype(bf16), "q", [(0, 1), (1, 0)]).astype(f32)
    total = mine + other
    gate_pre = total[:, :hidden]
    up_pre = total[:, hidden : 2 * hidden]
    back_grad = total[:, 2 * hidden :]

    weight = lax.dynamic_index_in_dim(combine, p, 0, keepdims=False)[:, None]
    sig = jax.nn.sigmoid(gate_pre)
    activation = (gate_pre * sig * up_pre).astype(bf16)
    term = jnp.sum(activation.astype(f32) * back_grad, axis=1)
    d_act = weight * back_grad
    d_gate = (d_act * up_pre * sig * (1.0 + gate_pre * (1.0 - sig))).astype(bf16)
    d_up = (d_act * gate_pre * sig).astype(bf16)
    piece = lax.dot_general(d_gate, wg, (((1,), (1,)), ((), ())), preferred_element_type=f32)
    piece = piece + lax.dot_general(d_up, wu, (((1,), (1,)), ((), ())), preferred_element_type=f32)
    piece = piece.astype(bf16).reshape(capacity, 2, spread, part)
    piece = jnp.transpose(piece, (2, 0, 1, 3)).reshape(spread, capacity, 2 * part)
    high = lax.reduce_precision(term, 8, 7)
    extra = jnp.stack([high.astype(bf16), (term - high).astype(bf16)])
    extra = jnp.pad(extra, ((0, 14), (0, 0)))
    piece = jnp.concatenate(
        [piece, jnp.broadcast_to(extra[None], (spread,) + extra.shape)], axis=1
    )
    pieces = lax.all_to_all(piece, ("x", "c"), split_axis=0, concat_axis=0, tiled=True)
    summed = jnp.sum(pieces.astype(f32), axis=0)
    term_sum = summed[capacity] + summed[capacity + 1]
    summed = summed[:capacity].astype(bf16)

    back = lax.dot_general(
        place, summed, (((0,), (0,)), ((), ())), preferred_element_type=f32
    ).astype(bf16)
    back = jnp.transpose(back.reshape(groups, peer, 2, part), (2, 0, 1, 3))
    back = jnp.stack([jnp.where(q == i, back, jnp.zeros((), bf16)) for i in range(2)])
    returned = lax.all_to_all(
        back.reshape(4 * groups, peer * part),
        ("p", "q", "z"),
        split_axis=0,
        concat_axis=0,
        tiled=True,
    )
    returned = returned.reshape(2, 2, groups * peer, part)
    returned = lax.dynamic_index_in_dim(returned, p, 1, keepdims=False)
    grad_tokens = lax.dot_general(
        pick,
        returned.reshape(experts * peer, part),
        (((0,), (0,)), ((), ())),
        preferred_element_type=f32,
    ).astype(bf16)

    from_zero = lax.ppermute(term_sum, "q", [(0, 1)])
    term_sum = jnp.where(q == 0, term_sum, from_zero)
    term_other = lax.ppermute(term_sum, "p", [(0, 1), (1, 0)])
    grad_combine = jnp.stack(
        [jnp.where(p == 0, term_sum, term_other), jnp.where(p == 0, term_other, term_sum)]
    )

    scaled_out = (weight * rows_out.astype(f32)).astype(bf16)
    over_slots = (((0,), (0,)), ((), ()))
    grad_down = lax.dot_general(activation, scaled_out, over_slots, preferred_element_type=f32)
    grad_gate = lax.dot_general(rows_in, d_gate, over_slots, preferred_element_type=f32)
    grad_up = lax.dot_general(rows_in, d_up, over_slots, preferred_element_type=f32)
    return (
        grad_tokens,
        grad_gate.astype(bf16)[None],
        grad_up.astype(bf16)[None],
        grad_down.astype(bf16)[None],
        grad_combine,
    )


def solution(mesh):
    groups, lanes = mesh.devices.shape
    split = Mesh(
        mesh.devices.reshape(groups, 2, 2, lanes // 8, 2), ("z", "p", "q", "x", "c")
    )
    mp = ("p", "q", "x", "c")
    placed = (
        P("z", mp),
        P("z", mp),
        P("z", None, mp),
        P("z", None, mp),
        P("z", mp, None),
        P("z", None),
        P(),
    )
    return jax.shard_map(
        local,
        mesh=split,
        in_specs=placed,
        out_specs=(
            P("z", mp),
            P("z", None, mp),
            P("z", None, mp),
            P("z", mp, None),
            P("z", None),
        ),
        check_vma=False,
    )
```

```python
import jax
import jax.numpy as jnp
from jax import lax
from jax.sharding import Mesh
from jax.sharding import PartitionSpec as P


def local(x_tokens, cotangent, w_gate, w_up, w_down, combine, indices):
    bf16 = jnp.bfloat16
    f32 = jnp.float32
    groups = lax.axis_size("z")
    spread = lax.axis_size("x") * lax.axis_size("c")
    tok_dev, part = x_tokens.shape
    experts, capacity = indices.shape
    exp_dev = experts // groups
    peer = 2 * capacity // groups
    z = lax.axis_index("z")
    p = lax.axis_index("p")
    q = lax.axis_index("q")
    wg = w_gate[0]
    wu = w_up[0]
    wd = w_down[0]

    table = jnp.concatenate([x_tokens, cotangent], axis=1)
    table = lax.ppermute(table, ("p", "q"), [(0, 0), (1, 2), (2, 1), (3, 3)])

    swap = [(0, 1), (1, 0)]
    wg_far = lax.ppermute(wg, "q", swap)
    wu_far = lax.ppermute(wu, "q", swap)
    wd_far = lax.ppermute(wd, "q", swap)

    slots = jnp.arange(capacity, dtype=jnp.int32)
    places = jnp.arange(peer, dtype=jnp.int32)
    tokens = jnp.arange(tok_dev, dtype=jnp.int32)
    ordered = jnp.transpose(indices.reshape(groups, exp_dev, capacity), (1, 0, 2)).reshape(
        experts, capacity
    )
    base = z * tok_dev
    start = jnp.sum(((ordered >= 0) & (ordered < base)).astype(jnp.int32), axis=1)
    want = start[:, None] + places[None, :]
    shifted = jnp.where(ordered >= 0, ordered - base + 1, 0)
    chosen = (
        jnp.sum(jnp.where(slots[None, None, :] == want[:, :, None], shifted[:, None, :], 0), axis=2)
        - 1
    )
    pick = (chosen[:, :, None] == tokens[None, None, :]).astype(bf16)
    pick = pick.reshape(experts * peer, tok_dev)
    send = jnp.dot(pick, table, preferred_element_type=f32).astype(bf16)
    recv = lax.all_to_all(
        send.reshape(experts, peer, 2 * part), ("p", "z"), split_axis=0, concat_axis=0, tiled=True
    )

    own = lax.dynamic_slice_in_dim(indices, z * exp_dev, exp_dev, 0)
    cells = jnp.arange(groups * peer, dtype=jnp.int32)
    cell_block = cells // peer
    earlier = (own[:, None, :] >= 0) & (own[:, None, :] < cell_block[None, :, None] * tok_dev)
    own_want = jnp.sum(earlier.astype(jnp.int32), axis=2) + cells % peer
    own_block = jnp.where(own >= 0, own // tok_dev, -1)
    place = jnp.where(own_block[:, :, None] == cell_block[None, None, :], own_want[:, None, :], -1)
    place = (place == slots[None, :, None]).astype(bf16)
    own_place = lax.dynamic_index_in_dim(place, p, 0, keepdims=False)
    recv, wg_far, wu_far, wd_far = lax.optimization_barrier((recv, wg_far, wu_far, wd_far))
    recv = recv.reshape(2, groups * peer, 2 * part)
    taken = [jnp.dot(own_place, recv[i], preferred_element_type=f32).astype(bf16) for i in range(2)]
    compact = jnp.concatenate(
        [taken[0][:, :part], taken[1][:, :part], taken[0][:, part:], taken[1][:, part:]], axis=1
    )
    half_cap = capacity // 2
    compact = compact.reshape(2, 1, half_cap, 4 * part)
    spreadout = jnp.broadcast_to(compact, (2, spread, half_cap, 4 * part))
    gathered = lax.all_to_all(
        spreadout.reshape(2 * spread, half_cap, 4 * part),
        ("q", "x", "c"),
        split_axis=0,
        concat_axis=0,
        tiled=True,
    ).reshape(2, spread, half_cap, 2, 2, part)

    def natural(block):
        return jnp.transpose(block, (2, 1, 3, 0, 4)).reshape(2, half_cap, 2 * spread * part)

    mine = natural(lax.dynamic_index_in_dim(gathered, q, 0, keepdims=False))
    theirs = natural(lax.dynamic_index_in_dim(gathered, 1 - q, 0, keepdims=False))

    def rows_by(first, second):
        return jnp.dot(mine[0], first, preferred_element_type=f32) + jnp.dot(
            theirs[0], second, preferred_element_type=f32
        )

    across = (((1,), (1,)), ((), ()))
    gate_pre = rows_by(wg, wg_far)
    up_pre = rows_by(wu, wu_far)
    back_grad = lax.dot_general(mine[1], wd, across, preferred_element_type=f32)
    back_grad = back_grad + lax.dot_general(theirs[1], wd_far, across, preferred_element_type=f32)

    weight = lax.dynamic_slice(combine, (p, q * half_cap), (1, half_cap)).reshape(half_cap, 1)
    sig = jax.nn.sigmoid(gate_pre)
    activation = (gate_pre * sig * up_pre).astype(bf16)
    term = jnp.sum(activation.astype(f32) * back_grad, axis=1)
    d_act = weight * back_grad
    d_gate = (d_act * up_pre * sig * (1.0 + gate_pre * (1.0 - sig))).astype(bf16)
    d_up = (d_act * gate_pre * sig).astype(bf16)

    def pieces_of(first, second):
        piece = lax.dot_general(d_gate, first, across, preferred_element_type=f32)
        piece = piece + lax.dot_general(d_up, second, across, preferred_element_type=f32)
        piece = piece.astype(bf16).reshape(2, half_cap // 2, 2, spread, part)
        piece = jnp.transpose(piece, (2, 3, 1, 0, 4))
        return piece.reshape(2 * spread, half_cap // 2, 2 * part)

    near = pieces_of(wg, wu)
    far = pieces_of(wg_far, wu_far)
    piece = jnp.concatenate([jnp.where(q == 0, near, far), jnp.where(q == 0, far, near)], axis=0)
    high = lax.reduce_precision(term, 8, 7)
    extra = jnp.concatenate([high.astype(bf16), (term - high).astype(bf16)]).reshape(1, 2 * half_cap)
    extra = jnp.pad(extra, ((0, 7), (0, 0)))
    piece = jnp.concatenate(
        [piece, jnp.broadcast_to(extra[None], (4 * spread,) + extra.shape)], axis=1
    )
    pieces = lax.all_to_all(piece, ("p", "q", "x", "c"), split_axis=0, concat_axis=0, tiled=True)
    pieces = pieces.reshape(2, 2, spread, half_cap // 2 + 8, 2 * part)
    summed = jnp.sum(pieces.astype(f32), axis=2)
    term_sum = summed[:, :, half_cap // 2]
    grad_combine = (term_sum[:, :, :half_cap] + term_sum[:, :, half_cap:]).reshape(
        exp_dev, capacity
    )
    summed = summed[:, :, : half_cap // 2].astype(bf16)
    summed = jnp.transpose(
        summed.reshape(exp_dev, 2, half_cap // 2, 2, part), (0, 1, 3, 2, 4)
    ).reshape(exp_dev, capacity, part)

    over_slots = (((0,), (0,)), ((), ()))
    back = jnp.concatenate(
        [
            lax.dot_general(place[i], summed[i], over_slots, preferred_element_type=f32).astype(bf16)
            for i in range(exp_dev)
        ],
        axis=1,
    )
    returned = lax.all_to_all(
        back.reshape(groups, peer, exp_dev * part), "z", split_axis=0, concat_axis=0, tiled=True
    ).reshape(groups * peer, exp_dev * part)
    pick = pick.reshape(exp_dev, groups * peer, tok_dev)
    grad_tokens = lax.dot_general(
        pick[0], returned[:, :part], over_slots, preferred_element_type=f32
    )
    grad_tokens = grad_tokens + lax.dot_general(
        pick[1], returned[:, part:], over_slots, preferred_element_type=f32
    )

    def scaled(rows):
        return (weight * rows.astype(f32)).astype(bf16)

    give = jnp.concatenate([theirs[0], scaled(theirs[1]), activation, d_gate, d_up], axis=1)
    got = lax.ppermute(give, "q", swap)
    keep = jnp.concatenate([mine[0], scaled(mine[1]), activation, d_gate, d_up], axis=1)
    both = jnp.concatenate([keep, got], axis=0)
    width = mine.shape[2]
    hidden = wg.shape[1]
    rows_in = both[:, :width]
    scaled_out = both[:, width : 2 * width]
    activation = both[:, 2 * width : 2 * width + hidden]
    d_gate = both[:, 2 * width + hidden : 2 * width + 2 * hidden]
    d_up = both[:, 2 * width + 2 * hidden :]
    grad_down = lax.dot_general(activation, scaled_out, over_slots, preferred_element_type=f32)
    grad_gate = lax.dot_general(rows_in, d_gate, over_slots, preferred_element_type=f32)
    grad_up = lax.dot_general(rows_in, d_up, over_slots, preferred_element_type=f32)
    return (
        grad_tokens.astype(bf16),
        grad_gate.astype(bf16)[None],
        grad_up.astype(bf16)[None],
        grad_down.astype(bf16)[None],
        grad_combine,
    )


def solution(mesh):
    groups, lanes = mesh.devices.shape
    split = Mesh(
        mesh.devices.reshape(groups, 2, 2, lanes // 8, 2), ("z", "p", "q", "x", "c")
    )
    mp = ("p", "q", "x", "c")
    placed = (
        P("z", mp),
        P("z", mp),
        P("z", None, mp),
        P("z", None, mp),
        P("z", mp, None),
        P("z", None),
        P(),
    )
    return jax.shard_map(
        local,
        mesh=split,
        in_specs=placed,
        out_specs=(
            P("z", mp),
            P("z", None, mp),
            P("z", None, mp),
            P("z", mp, None),
            P("z", None),
        ),
        check_vma=False,
    )
```

```python
import jax
import jax.numpy as jnp
from jax import lax
from jax.experimental import pallas as pl
from jax.experimental.pallas import tpu as pltpu
from jax.sharding import Mesh
from jax.sharding import PartitionSpec as P


def middle(
    q_ref,
    weight_ref,
    rows_ref,
    wg_far,
    wu_far,
    wd_far,
    out_ref,
    keep_ref,
    give_ref,
    nat_ref,
    wg_ref,
    wu_ref,
    wd_ref,
    sem,
):
    loads = [
        pltpu.make_async_copy(far, near, sem.at[i])
        for i, (far, near) in enumerate(((wg_far, wg_ref), (wu_far, wu_ref), (wd_far, wd_ref)))
    ]
    for load in loads:
        load.start()
    bf16 = jnp.bfloat16
    f32 = jnp.float32
    q = q_ref[0]
    spread = rows_ref.shape[0] // 2
    slots = rows_ref.shape[1]
    width = wg_ref.shape[1]
    hidden = wg_ref.shape[2]
    weight = weight_ref[...]
    low = lax.broadcasted_iota(jnp.int32, (slots, 128), 1) < 64

    def halves(first, second):
        return (
            jnp.where(low[: first.shape[0]], first, pltpu.roll(second, 64, 1)),
            jnp.where(low[: first.shape[0]], pltpu.roll(first, 64, 1), second),
        )

    for side in range(2):
        for kind in range(2):
            for i in range(spread // 2):
                lanes = pl.ds(kind * 128, 128)
                first = rows_ref[side * spread + 2 * i, :, lanes].astype(f32)
                second = rows_ref[side * spread + 2 * i + 1, :, lanes].astype(f32)
                for a, part in enumerate(halves(first, second)):
                    at = kind * width + a * (width // 2) + i * 128
                    nat_ref[side, :, pl.ds(at, 128)] = part.astype(bf16)

    def over(side, kind):
        return nat_ref[side, :, pl.ds(kind * width, width)]

    across = (((1,), (1,)), ((), ()))
    loads[0].wait()
    gate_pre = jnp.dot(over(0, 0), wg_ref[0], preferred_element_type=f32)
    gate_pre = gate_pre + jnp.dot(over(1, 0), wg_ref[1], preferred_element_type=f32)
    loads[1].wait()
    up_pre = jnp.dot(over(0, 0), wu_ref[0], preferred_element_type=f32)
    up_pre = up_pre + jnp.dot(over(1, 0), wu_ref[1], preferred_element_type=f32)
    loads[2].wait()
    back_grad = lax.dot_general(over(0, 1), wd_ref[0], across, preferred_element_type=f32)
    back_grad = back_grad + lax.dot_general(
        over(1, 1), wd_ref[1], across, preferred_element_type=f32
    )
    sig = 1.0 / (1.0 + jnp.exp(-gate_pre))
    activation = (gate_pre * sig * up_pre).astype(bf16)
    term = jnp.sum(activation.astype(f32) * back_grad, axis=1, keepdims=True)
    d_act = weight * back_grad
    d_gate = (d_act * up_pre * sig * (1.0 + gate_pre * (1.0 - sig))).astype(bf16)
    d_up = (d_act * gate_pre * sig).astype(bf16)

    lane = lax.broadcasted_iota(jnp.int32, (slots, 128), 1)
    slot = lax.broadcasted_iota(jnp.int32, (slots, 128), 0)
    line = jnp.sum(jnp.where((lane & 63) == slot, term, 0.0), axis=0, keepdims=True)
    rounded = line.astype(bf16).astype(f32)
    line = jnp.where(low[:1], rounded, line - rounded)
    extra = jnp.where(slot[:16] == 0, line, 0.0).astype(bf16)
    half = slots // 2
    for side in range(2):
        piece = lax.dot_general(d_gate, wg_ref[side], across, preferred_element_type=f32)
        piece = piece + lax.dot_general(d_up, wu_ref[side], across, preferred_element_type=f32)
        for a in range(2):
            for i in range(spread // 2):
                at = a * (width // 2) + i * 128
                top, bottom = piece[:half, at : at + 128], piece[half:, at : at + 128]
                for j, part in enumerate(halves(top, bottom)):
                    to = (side * 2 + a) * spread + 2 * i + j
                    out_ref[to, pl.ds(0, half), :] = part.astype(bf16)
                    out_ref[to, pl.ds(half, 16), :] = extra

    for ref, side in ((keep_ref, q), (give_ref, 1 - q)):
        ref[:, pl.ds(0, width)] = nat_ref[side, :, pl.ds(0, width)]
        rows_out = nat_ref[side, :, pl.ds(width, width)].astype(f32)
        ref[:, pl.ds(width, width)] = (weight * rows_out).astype(bf16)
        ref[:, pl.ds(2 * width, hidden)] = activation
        ref[:, pl.ds(2 * width + hidden, hidden)] = d_gate
        ref[:, pl.ds(2 * width + 2 * hidden, hidden)] = d_up


def local(x_tokens, cotangent, w_gate, w_up, w_down, combine, indices):
    bf16 = jnp.bfloat16
    f32 = jnp.float32
    groups = lax.axis_size("z")
    spread = lax.axis_size("x") * lax.axis_size("c")
    tok_dev, part = x_tokens.shape
    experts, capacity = indices.shape
    exp_dev = experts // groups
    peer = 2 * capacity // groups
    z = lax.axis_index("z")
    p = lax.axis_index("p")
    q = lax.axis_index("q")
    wg = w_gate[0]
    wu = w_up[0]
    wd = w_down[0]

    table = jnp.concatenate([x_tokens, cotangent], axis=1)
    table = lax.ppermute(table, ("p", "q"), [(0, 0), (1, 2), (2, 1), (3, 3)])

    wg_both = lax.all_gather(wg, "q", axis=0)
    wu_both = lax.all_gather(wu, "q", axis=0)
    wd_both = lax.all_gather(wd, "q", axis=0)

    slots = jnp.arange(capacity, dtype=jnp.int32)
    places = jnp.arange(peer, dtype=jnp.int32)
    tokens = jnp.arange(tok_dev, dtype=jnp.int32)
    ordered = jnp.transpose(indices.reshape(groups, exp_dev, capacity), (1, 0, 2)).reshape(
        experts, capacity
    )
    base = z * tok_dev
    start = jnp.sum(((ordered >= 0) & (ordered < base)).astype(jnp.int32), axis=1)
    want = start[:, None] + places[None, :]
    shifted = jnp.where(ordered >= 0, ordered - base + 1, 0)
    chosen = (
        jnp.sum(jnp.where(slots[None, None, :] == want[:, :, None], shifted[:, None, :], 0), axis=2)
        - 1
    )
    pick = (chosen[:, :, None] == tokens[None, None, :]).astype(bf16)
    pick = pick.reshape(experts * peer, tok_dev)
    send = jnp.dot(pick, table, preferred_element_type=f32).astype(bf16)
    recv = lax.all_to_all(
        send.reshape(experts, peer, 2 * part), ("p", "z"), split_axis=0, concat_axis=0, tiled=True
    )

    own = lax.dynamic_slice_in_dim(indices, z * exp_dev, exp_dev, 0)
    cells = jnp.arange(groups * peer, dtype=jnp.int32)
    cell_block = cells // peer
    earlier = (own[:, None, :] >= 0) & (own[:, None, :] < cell_block[None, :, None] * tok_dev)
    own_want = jnp.sum(earlier.astype(jnp.int32), axis=2) + cells % peer
    own_block = jnp.where(own >= 0, own // tok_dev, -1)
    place = jnp.where(own_block[:, :, None] == cell_block[None, None, :], own_want[:, None, :], -1)
    place = (place == slots[None, :, None]).astype(bf16)
    own_place = lax.dynamic_index_in_dim(place, p, 0, keepdims=False)
    recv = recv.reshape(2, groups * peer, 2 * part)
    taken = [jnp.dot(own_place, recv[i], preferred_element_type=f32).astype(bf16) for i in range(2)]
    compact = jnp.concatenate(
        [taken[0][:, :part], taken[1][:, :part], taken[0][:, part:], taken[1][:, part:]], axis=1
    )
    half_cap = capacity // 2
    compact = compact.reshape(2, 1, half_cap, 4 * part)
    spreadout = jnp.broadcast_to(compact, (2, spread, half_cap, 4 * part))
    gathered = lax.all_to_all(
        spreadout.reshape(2 * spread, half_cap, 4 * part),
        ("q", "x", "c"),
        split_axis=0,
        concat_axis=0,
        tiled=True,
    )
    hidden = wg.shape[1]
    width = wg.shape[0]
    weight = lax.dynamic_slice(combine, (p, q * half_cap), (1, half_cap)).reshape(half_cap, 1)
    vmem = pl.BlockSpec(memory_space=pltpu.VMEM)
    held = jax.ShapeDtypeStruct((half_cap, 2 * width + 3 * hidden), bf16)
    piece, keep, give = pl.pallas_call(
        middle,
        out_shape=(
            jax.ShapeDtypeStruct((4 * spread, half_cap // 2 + 16, 2 * part), bf16),
            held,
            held,
        ),
        in_specs=[pl.BlockSpec(memory_space=pltpu.SMEM)] + [vmem] * 2
        + [pl.BlockSpec(memory_space=pltpu.HBM)] * 3,
        out_specs=(vmem, vmem, vmem),
        scratch_shapes=[
            pltpu.VMEM((2, half_cap, 2 * width), bf16),
            pltpu.VMEM(wg_both.shape, bf16),
            pltpu.VMEM(wu_both.shape, bf16),
            pltpu.VMEM(wd_both.shape, bf16),
            pltpu.SemaphoreType.DMA((3,)),
        ],
        compiler_params=pltpu.CompilerParams(vmem_limit_bytes=52 * 1024 * 1024),
        cost_estimate=pl.CostEstimate(
            flops=20 * half_cap * width * hidden, bytes_accessed=5 << 20, transcendentals=0
        ),
    )(q.reshape(1), weight, gathered, wg_both, wu_both, wd_both)
    pieces = lax.all_to_all(piece, ("p", "q", "x", "c"), split_axis=0, concat_axis=0, tiled=True)
    pieces = pieces.reshape(2, 2, spread, half_cap // 2 + 16, 2 * part)
    summed = jnp.sum(pieces.astype(f32), axis=2)
    term_sum = summed[:, :, half_cap // 2]
    grad_combine = (term_sum[:, :, :half_cap] + term_sum[:, :, half_cap:]).reshape(
        exp_dev, capacity
    )
    summed = summed[:, :, : half_cap // 2].astype(bf16)
    summed = jnp.transpose(
        summed.reshape(exp_dev, 2, half_cap // 2, 2, part), (0, 1, 3, 2, 4)
    ).reshape(exp_dev, capacity, part)

    over_slots = (((0,), (0,)), ((), ()))
    back = jnp.concatenate(
        [
            lax.dot_general(place[i], summed[i], over_slots, preferred_element_type=f32).astype(bf16)
            for i in range(exp_dev)
        ],
        axis=1,
    )
    returned = lax.all_to_all(
        back.reshape(groups, peer, exp_dev * part), "z", split_axis=0, concat_axis=0, tiled=True
    ).reshape(groups * peer, exp_dev * part)
    pick = pick.reshape(exp_dev, groups * peer, tok_dev)
    grad_tokens = lax.dot_general(
        pick[0], returned[:, :part], over_slots, preferred_element_type=f32
    )
    grad_tokens = grad_tokens + lax.dot_general(
        pick[1], returned[:, part:], over_slots, preferred_element_type=f32
    )

    give, _ = lax.optimization_barrier((give, back))
    got = lax.all_gather(give, "q", axis=0)
    got = lax.dynamic_index_in_dim(got, 1 - q, 0, keepdims=False)
    both = jnp.concatenate([keep, got], axis=0)
    rows_in = both[:, :width]
    scaled_out = both[:, width : 2 * width]
    activation = both[:, 2 * width : 2 * width + hidden]
    d_gate = both[:, 2 * width + hidden : 2 * width + 2 * hidden]
    d_up = both[:, 2 * width + 2 * hidden :]
    grad_down = lax.dot_general(activation, scaled_out, over_slots, preferred_element_type=f32)
    grad_gate = lax.dot_general(rows_in, d_gate, over_slots, preferred_element_type=f32)
    grad_up = lax.dot_general(rows_in, d_up, over_slots, preferred_element_type=f32)
    return (
        grad_tokens.astype(bf16),
        grad_gate.astype(bf16)[None],
        grad_up.astype(bf16)[None],
        grad_down.astype(bf16)[None],
        grad_combine,
    )


def solution(mesh):
    groups, lanes = mesh.devices.shape
    split = Mesh(
        mesh.devices.reshape(groups, 2, 2, lanes // 8, 2), ("z", "p", "q", "x", "c")
    )
    mp = ("p", "q", "x", "c")
    placed = (
        P("z", mp),
        P("z", mp),
        P("z", None, mp),
        P("z", None, mp),
        P("z", mp, None),
        P("z", None),
        P(),
    )
    return jax.shard_map(
        local,
        mesh=split,
        in_specs=placed,
        out_specs=(
            P("z", mp),
            P("z", None, mp),
            P("z", None, mp),
            P("z", mp, None),
            P("z", None),
        ),
        check_vma=False,
    )
```

```python
import jax
import jax.numpy as jnp
from jax import lax
from jax.experimental import pallas as pl
from jax.experimental.pallas import tpu as pltpu
from jax.sharding import Mesh
from jax.sharding import PartitionSpec as P


def middle(
    q_ref,
    weight_ref,
    rows_ref,
    wg_own,
    wu_own,
    wd_own,
    wg_far,
    wu_far,
    wd_far,
    out_ref,
    keep_ref,
    give_ref,
    nat_ref,
    wg_ref,
    wu_ref,
    wd_ref,
    sem,
):
    q = q_ref[0]
    loads = []
    for i, (own, far, near) in enumerate(
        ((wg_own, wg_far, wg_ref), (wu_own, wu_far, wu_ref), (wd_own, wd_far, wd_ref))
    ):
        loads.append(
            (
                pltpu.make_async_copy(own, near.at[q], sem.at[2 * i]),
                pltpu.make_async_copy(far, near.at[1 - q], sem.at[2 * i + 1]),
            )
        )
        loads[i][0].start()
        loads[i][1].start()
    bf16 = jnp.bfloat16
    f32 = jnp.float32
    spread = rows_ref.shape[0] // 2
    slots = rows_ref.shape[1]
    width = wg_ref.shape[1]
    hidden = wg_ref.shape[2]
    weight = weight_ref[...]
    low = lax.broadcasted_iota(jnp.int32, (slots, 128), 1) < 64

    def halves(first, second):
        return (
            jnp.where(low[: first.shape[0]], first, pltpu.roll(second, 64, 1)),
            jnp.where(low[: first.shape[0]], pltpu.roll(first, 64, 1), second),
        )

    for side in range(2):
        for kind in range(2):
            for i in range(spread // 2):
                lanes = pl.ds(kind * 128, 128)
                first = rows_ref[side * spread + 2 * i, :, lanes].astype(f32)
                second = rows_ref[side * spread + 2 * i + 1, :, lanes].astype(f32)
                for a, part in enumerate(halves(first, second)):
                    at = kind * width + a * (width // 2) + i * 128
                    nat_ref[side, :, pl.ds(at, 128)] = part.astype(bf16)

    def over(side, kind):
        return nat_ref[side, :, pl.ds(kind * width, width)]

    across = (((1,), (1,)), ((), ()))
    loads[0][0].wait()
    loads[0][1].wait()
    gate_pre = jnp.dot(over(0, 0), wg_ref[0], preferred_element_type=f32)
    gate_pre = gate_pre + jnp.dot(over(1, 0), wg_ref[1], preferred_element_type=f32)
    loads[1][0].wait()
    loads[1][1].wait()
    up_pre = jnp.dot(over(0, 0), wu_ref[0], preferred_element_type=f32)
    up_pre = up_pre + jnp.dot(over(1, 0), wu_ref[1], preferred_element_type=f32)
    loads[2][0].wait()
    loads[2][1].wait()
    back_grad = lax.dot_general(over(0, 1), wd_ref[0], across, preferred_element_type=f32)
    back_grad = back_grad + lax.dot_general(
        over(1, 1), wd_ref[1], across, preferred_element_type=f32
    )
    sig = 1.0 / (1.0 + jnp.exp(-gate_pre))
    activation = (gate_pre * sig * up_pre).astype(bf16)
    term = jnp.sum(activation.astype(f32) * back_grad, axis=1, keepdims=True)
    d_act = weight * back_grad
    d_gate = (d_act * up_pre * sig * (1.0 + gate_pre * (1.0 - sig))).astype(bf16)
    d_up = (d_act * gate_pre * sig).astype(bf16)

    lane = lax.broadcasted_iota(jnp.int32, (slots, 128), 1)
    slot = lax.broadcasted_iota(jnp.int32, (slots, 128), 0)
    line = jnp.sum(jnp.where((lane & 63) == slot, term, 0.0), axis=0, keepdims=True)
    rounded = line.astype(bf16).astype(f32)
    line = jnp.where(low[:1], rounded, line - rounded)
    extra = jnp.where(slot[:16] == 0, line, 0.0).astype(bf16)
    half = slots // 2
    for side in range(2):
        piece = lax.dot_general(d_gate, wg_ref[side], across, preferred_element_type=f32)
        piece = piece + lax.dot_general(d_up, wu_ref[side], across, preferred_element_type=f32)
        for a in range(2):
            for i in range(spread // 2):
                at = a * (width // 2) + i * 128
                top, bottom = piece[:half, at : at + 128], piece[half:, at : at + 128]
                for j, part in enumerate(halves(top, bottom)):
                    to = (side * 2 + a) * spread + 2 * i + j
                    out_ref[to, pl.ds(0, half), :] = part.astype(bf16)
                    out_ref[to, pl.ds(half, 16), :] = extra

    for ref, side in ((keep_ref, q), (give_ref, 1 - q)):
        ref[:, pl.ds(0, width)] = nat_ref[side, :, pl.ds(0, width)]
        rows_out = nat_ref[side, :, pl.ds(width, width)].astype(f32)
        ref[:, pl.ds(width, width)] = (weight * rows_out).astype(bf16)
        ref[:, pl.ds(2 * width, hidden)] = activation
        ref[:, pl.ds(2 * width + hidden, hidden)] = d_gate
        ref[:, pl.ds(2 * width + 2 * hidden, hidden)] = d_up


def local(x_tokens, cotangent, w_gate, w_up, w_down, combine, indices):
    bf16 = jnp.bfloat16
    f32 = jnp.float32
    groups = lax.axis_size("z")
    spread = lax.axis_size("x") * lax.axis_size("c")
    tok_dev, part = x_tokens.shape
    experts, capacity = indices.shape
    exp_dev = experts // groups
    peer = 2 * capacity // groups
    z = lax.axis_index("z")
    p = lax.axis_index("p")
    q = lax.axis_index("q")
    wg = w_gate[0]
    wu = w_up[0]
    wd = w_down[0]

    table = jnp.concatenate([x_tokens, cotangent], axis=1)
    table = lax.ppermute(table, ("p", "q"), [(0, 0), (1, 2), (2, 1), (3, 3)])

    swap = [(0, 1), (1, 0)]

    slots = jnp.arange(capacity, dtype=jnp.int32)
    places = jnp.arange(peer, dtype=jnp.int32)
    tokens = jnp.arange(tok_dev, dtype=jnp.int32)
    ordered = jnp.transpose(indices.reshape(groups, exp_dev, capacity), (1, 0, 2)).reshape(
        experts, capacity
    )
    base = z * tok_dev
    start = jnp.sum(((ordered >= 0) & (ordered < base)).astype(jnp.int32), axis=1)
    want = start[:, None] + places[None, :]
    shifted = jnp.where(ordered >= 0, ordered - base + 1, 0)
    chosen = (
        jnp.sum(jnp.where(slots[None, None, :] == want[:, :, None], shifted[:, None, :], 0), axis=2)
        - 1
    )
    pick = (chosen[:, :, None] == tokens[None, None, :]).astype(bf16)
    pick = pick.reshape(experts * peer, tok_dev)
    send = jnp.dot(pick, table, preferred_element_type=f32).astype(bf16)
    send, wg_give, wu_give = lax.optimization_barrier((send, wg, wu))
    wg_far = lax.ppermute(wg_give, "q", swap)
    wu_far = lax.ppermute(wu_give, "q", swap)
    recv = lax.all_to_all(
        send.reshape(experts, peer, 2 * part), ("p", "z"), split_axis=0, concat_axis=0, tiled=True
    )

    own = lax.dynamic_slice_in_dim(indices, z * exp_dev, exp_dev, 0)
    cells = jnp.arange(groups * peer, dtype=jnp.int32)
    cell_block = cells // peer
    earlier = (own[:, None, :] >= 0) & (own[:, None, :] < cell_block[None, :, None] * tok_dev)
    own_want = jnp.sum(earlier.astype(jnp.int32), axis=2) + cells % peer
    own_block = jnp.where(own >= 0, own // tok_dev, -1)
    place = jnp.where(own_block[:, :, None] == cell_block[None, None, :], own_want[:, None, :], -1)
    place = (place == slots[None, :, None]).astype(bf16)
    own_place = lax.dynamic_index_in_dim(place, p, 0, keepdims=False)
    recv, wg_far, wu_far = lax.optimization_barrier((recv, wg_far, wu_far))
    recv = recv.reshape(2, groups * peer, 2 * part)
    taken = [jnp.dot(own_place, recv[i], preferred_element_type=f32).astype(bf16) for i in range(2)]
    compact = jnp.concatenate(
        [taken[0][:, :part], taken[1][:, :part], taken[0][:, part:], taken[1][:, part:]], axis=1
    )
    half_cap = capacity // 2
    compact = compact.reshape(2, 1, half_cap, 4 * part)
    spreadout = jnp.broadcast_to(compact, (2, spread, half_cap, 4 * part))
    wd_far = lax.ppermute(wd, "q", swap)
    gathered = lax.all_to_all(
        spreadout.reshape(2 * spread, half_cap, 4 * part),
        ("q", "x", "c"),
        split_axis=0,
        concat_axis=0,
        tiled=True,
    )
    hidden = wg.shape[1]
    width = wg.shape[0]
    weight = lax.dynamic_slice(combine, (p, q * half_cap), (1, half_cap)).reshape(half_cap, 1)
    vmem = pl.BlockSpec(memory_space=pltpu.VMEM)
    held = jax.ShapeDtypeStruct((half_cap, 2 * width + 3 * hidden), bf16)
    piece, keep, give = pl.pallas_call(
        middle,
        out_shape=(
            jax.ShapeDtypeStruct((4 * spread, half_cap // 2 + 16, 2 * part), bf16),
            held,
            held,
        ),
        in_specs=[pl.BlockSpec(memory_space=pltpu.SMEM)] + [vmem] * 2
        + [pl.BlockSpec(memory_space=pltpu.HBM)] * 6,
        out_specs=(vmem, vmem, vmem),
        scratch_shapes=[
            pltpu.VMEM((2, half_cap, 2 * width), bf16),
            pltpu.VMEM((2,) + wg.shape, bf16),
            pltpu.VMEM((2,) + wu.shape, bf16),
            pltpu.VMEM((2,) + wd.shape, bf16),
            pltpu.SemaphoreType.DMA((6,)),
        ],
        compiler_params=pltpu.CompilerParams(vmem_limit_bytes=52 * 1024 * 1024),
        cost_estimate=pl.CostEstimate(
            flops=20 * half_cap * width * hidden, bytes_accessed=5 << 20, transcendentals=0
        ),
    )(q.reshape(1), weight, gathered, wg, wu, wd, wg_far, wu_far, wd_far)
    pieces = lax.all_to_all(piece, ("p", "q", "x", "c"), split_axis=0, concat_axis=0, tiled=True)
    pieces = pieces.reshape(2, 2, spread, half_cap // 2 + 16, 2 * part)
    summed = jnp.sum(pieces.astype(f32), axis=2)
    term_sum = summed[:, :, half_cap // 2]
    grad_combine = (term_sum[:, :, :half_cap] + term_sum[:, :, half_cap:]).reshape(
        exp_dev, capacity
    )
    summed = summed[:, :, : half_cap // 2].astype(bf16)
    summed = jnp.transpose(
        summed.reshape(exp_dev, 2, half_cap // 2, 2, part), (0, 1, 3, 2, 4)
    ).reshape(exp_dev, capacity, part)

    over_slots = (((0,), (0,)), ((), ()))
    back = jnp.concatenate(
        [
            lax.dot_general(place[i], summed[i], over_slots, preferred_element_type=f32).astype(bf16)
            for i in range(exp_dev)
        ],
        axis=1,
    )
    returned = lax.all_to_all(
        back.reshape(groups, peer, exp_dev * part), "z", split_axis=0, concat_axis=0, tiled=True
    ).reshape(groups * peer, exp_dev * part)
    pick = pick.reshape(exp_dev, groups * peer, tok_dev)
    grad_tokens = lax.dot_general(
        pick[0], returned[:, :part], over_slots, preferred_element_type=f32
    )
    grad_tokens = grad_tokens + lax.dot_general(
        pick[1], returned[:, part:], over_slots, preferred_element_type=f32
    )

    give, _ = lax.optimization_barrier((give, back))
    got = lax.all_gather(give, "q", axis=0)
    got = lax.dynamic_index_in_dim(got, 1 - q, 0, keepdims=False)
    both = jnp.concatenate([keep, got], axis=0)
    rows_in = both[:, :width]
    scaled_out = both[:, width : 2 * width]
    activation = both[:, 2 * width : 2 * width + hidden]
    d_gate = both[:, 2 * width + hidden : 2 * width + 2 * hidden]
    d_up = both[:, 2 * width + 2 * hidden :]
    grad_down = lax.dot_general(activation, scaled_out, over_slots, preferred_element_type=f32)
    grad_gate = lax.dot_general(rows_in, d_gate, over_slots, preferred_element_type=f32)
    grad_up = lax.dot_general(rows_in, d_up, over_slots, preferred_element_type=f32)
    return (
        grad_tokens.astype(bf16),
        grad_gate.astype(bf16)[None],
        grad_up.astype(bf16)[None],
        grad_down.astype(bf16)[None],
        grad_combine,
    )


def solution(mesh):
    groups, lanes = mesh.devices.shape
    split = Mesh(
        mesh.devices.reshape(groups, 2, 2, lanes // 8, 2), ("z", "p", "q", "x", "c")
    )
    mp = ("p", "q", "x", "c")
    placed = (
        P("z", mp),
        P("z", mp),
        P("z", None, mp),
        P("z", None, mp),
        P("z", mp, None),
        P("z", None),
        P(),
    )
    return jax.shard_map(
        local,
        mesh=split,
        in_specs=placed,
        out_specs=(
            P("z", mp),
            P("z", None, mp),
            P("z", None, mp),
            P("z", mp, None),
            P("z", None),
        ),
        check_vma=False,
    )
```

```python
import jax
import jax.numpy as jnp
from jax import lax
from jax.experimental import pallas as pl
from jax.experimental.pallas import tpu as pltpu
from jax.sharding import Mesh
from jax.sharding import PartitionSpec as P


def middle(
    q_ref,
    weight_ref,
    rows_ref,
    wg_own,
    wu_own,
    wd_own,
    far_ref,
    out_ref,
    keep_ref,
    give_ref,
    nat_ref,
    wg_ref,
    wu_ref,
    wd_ref,
    sem,
):
    q = q_ref[0]
    chunk = wg_own.shape[1]
    far = 1 - q
    pairs = [
        [(wg_own, wg_ref.at[q]), (far_ref.at[0], wg_ref.at[far])],
        [(wu_own, wu_ref.at[q]), (far_ref.at[1], wu_ref.at[far])],
        [(wd_own, wd_ref.at[q])]
        + [
            (far_ref.at[2, pl.ds(i * chunk, chunk)], wd_ref.at[far, :, pl.ds(i * chunk, chunk)])
            for i in range(wd_own.shape[1] // chunk)
        ],
    ]
    loads = []
    count = 0
    for group in pairs:
        loads.append([])
        for source, target in group:
            loads[-1].append(pltpu.make_async_copy(source, target, sem.at[count]))
            loads[-1][-1].start()
            count += 1
    bf16 = jnp.bfloat16
    f32 = jnp.float32
    spread = rows_ref.shape[0] // 2
    slots = rows_ref.shape[1]
    width = wg_ref.shape[1]
    hidden = wg_ref.shape[2]
    weight = weight_ref[...]
    low = lax.broadcasted_iota(jnp.int32, (slots, 128), 1) < 64

    def halves(first, second):
        return (
            jnp.where(low[: first.shape[0]], first, pltpu.roll(second, 64, 1)),
            jnp.where(low[: first.shape[0]], pltpu.roll(first, 64, 1), second),
        )

    for side in range(2):
        for kind in range(2):
            for i in range(spread // 2):
                lanes = pl.ds(kind * 128, 128)
                first = rows_ref[side * spread + 2 * i, :, lanes].astype(f32)
                second = rows_ref[side * spread + 2 * i + 1, :, lanes].astype(f32)
                for a, part in enumerate(halves(first, second)):
                    at = kind * width + a * (width // 2) + i * 128
                    nat_ref[side, :, pl.ds(at, 128)] = part.astype(bf16)

    def over(side, kind):
        return nat_ref[side, :, pl.ds(kind * width, width)]

    across = (((1,), (1,)), ((), ()))
    for load in loads[0]:
        load.wait()
    gate_pre = jnp.dot(over(0, 0), wg_ref[0], preferred_element_type=f32)
    gate_pre = gate_pre + jnp.dot(over(1, 0), wg_ref[1], preferred_element_type=f32)
    for load in loads[1]:
        load.wait()
    up_pre = jnp.dot(over(0, 0), wu_ref[0], preferred_element_type=f32)
    up_pre = up_pre + jnp.dot(over(1, 0), wu_ref[1], preferred_element_type=f32)
    for load in loads[2]:
        load.wait()
    back_grad = lax.dot_general(over(0, 1), wd_ref[0], across, preferred_element_type=f32)
    back_grad = back_grad + lax.dot_general(
        over(1, 1), wd_ref[1], across, preferred_element_type=f32
    )
    sig = 1.0 / (1.0 + jnp.exp(-gate_pre))
    activation = (gate_pre * sig * up_pre).astype(bf16)
    term = jnp.sum(activation.astype(f32) * back_grad, axis=1, keepdims=True)
    d_act = weight * back_grad
    d_gate = (d_act * up_pre * sig * (1.0 + gate_pre * (1.0 - sig))).astype(bf16)
    d_up = (d_act * gate_pre * sig).astype(bf16)

    lane = lax.broadcasted_iota(jnp.int32, (slots, 128), 1)
    slot = lax.broadcasted_iota(jnp.int32, (slots, 128), 0)
    line = jnp.sum(jnp.where((lane & 63) == slot, term, 0.0), axis=0, keepdims=True)
    rounded = line.astype(bf16).astype(f32)
    line = jnp.where(low[:1], rounded, line - rounded)
    extra = jnp.where(slot[:16] == 0, line, 0.0).astype(bf16)
    half = slots // 2
    for side in range(2):
        piece = lax.dot_general(d_gate, wg_ref[side], across, preferred_element_type=f32)
        piece = piece + lax.dot_general(d_up, wu_ref[side], across, preferred_element_type=f32)
        for a in range(2):
            for i in range(spread // 2):
                at = a * (width // 2) + i * 128
                top, bottom = piece[:half, at : at + 128], piece[half:, at : at + 128]
                for j, part in enumerate(halves(top, bottom)):
                    to = (side * 2 + a) * spread + 2 * i + j
                    out_ref[to, pl.ds(0, half), :] = part.astype(bf16)
                    out_ref[to, pl.ds(half, 16), :] = extra

    for ref, side in ((keep_ref, q), (give_ref, 1 - q)):
        ref[:, pl.ds(0, width)] = nat_ref[side, :, pl.ds(0, width)]
        rows_out = nat_ref[side, :, pl.ds(width, width)].astype(f32)
        ref[:, pl.ds(width, width)] = (weight * rows_out).astype(bf16)
        ref[:, pl.ds(2 * width, hidden)] = activation
        ref[:, pl.ds(2 * width + hidden, hidden)] = d_gate
        ref[:, pl.ds(2 * width + 2 * hidden, hidden)] = d_up


def pack(wg_ref, wu_ref, wd_ref, out_ref, sem):
    chunk = wg_ref.shape[1]
    pairs = [(wg_ref, out_ref.at[0]), (wu_ref, out_ref.at[1])] + [
        (wd_ref.at[:, pl.ds(i * chunk, chunk)], out_ref.at[2, pl.ds(i * chunk, chunk)])
        for i in range(wd_ref.shape[1] // chunk)
    ]
    copies = [
        pltpu.make_async_copy(source, target, sem.at[i])
        for i, (source, target) in enumerate(pairs)
    ]
    for copy in copies:
        copy.start()
    for copy in copies:
        copy.wait()


def local(x_tokens, cotangent, w_gate, w_up, w_down, combine, indices):
    bf16 = jnp.bfloat16
    f32 = jnp.float32
    groups = lax.axis_size("z")
    spread = lax.axis_size("x") * lax.axis_size("c")
    tok_dev, part = x_tokens.shape
    experts, capacity = indices.shape
    exp_dev = experts // groups
    peer = 2 * capacity // groups
    z = lax.axis_index("z")
    p = lax.axis_index("p")
    q = lax.axis_index("q")
    wg = w_gate[0]
    wu = w_up[0]
    wd = w_down[0]

    table = jnp.concatenate([x_tokens, cotangent], axis=1)
    table = lax.ppermute(table, ("p", "q"), [(0, 0), (1, 2), (2, 1), (3, 3)])

    swap = [(0, 1), (1, 0)]
    here = pl.BlockSpec(memory_space=pltpu.HBM)
    packed = pl.pallas_call(
        pack,
        out_shape=jax.ShapeDtypeStruct((3,) + wg.shape, bf16),
        in_specs=[here] * 3,
        out_specs=here,
        scratch_shapes=[pltpu.SemaphoreType.DMA((6,))],
        cost_estimate=pl.CostEstimate(flops=0, bytes_accessed=3 << 20, transcendentals=0),
    )(wg, wu, wd)
    far = lax.ppermute(packed, "q", swap)

    slots = jnp.arange(capacity, dtype=jnp.int32)
    places = jnp.arange(peer, dtype=jnp.int32)
    tokens = jnp.arange(tok_dev, dtype=jnp.int32)
    ordered = jnp.transpose(indices.reshape(groups, exp_dev, capacity), (1, 0, 2)).reshape(
        experts, capacity
    )
    base = z * tok_dev
    start = jnp.sum(((ordered >= 0) & (ordered < base)).astype(jnp.int32), axis=1)
    want = start[:, None] + places[None, :]
    shifted = jnp.where(ordered >= 0, ordered - base + 1, 0)
    chosen = (
        jnp.sum(jnp.where(slots[None, None, :] == want[:, :, None], shifted[:, None, :], 0), axis=2)
        - 1
    )
    pick = (chosen[:, :, None] == tokens[None, None, :]).astype(bf16)
    pick = pick.reshape(experts * peer, tok_dev)
    send = jnp.dot(pick, table, preferred_element_type=f32).astype(bf16)
    recv = lax.all_to_all(
        send.reshape(experts, peer, 2 * part), ("p", "z"), split_axis=0, concat_axis=0, tiled=True
    )

    own = lax.dynamic_slice_in_dim(indices, z * exp_dev, exp_dev, 0)
    cells = jnp.arange(groups * peer, dtype=jnp.int32)
    cell_block = cells // peer
    earlier = (own[:, None, :] >= 0) & (own[:, None, :] < cell_block[None, :, None] * tok_dev)
    own_want = jnp.sum(earlier.astype(jnp.int32), axis=2) + cells % peer
    own_block = jnp.where(own >= 0, own // tok_dev, -1)
    place = jnp.where(own_block[:, :, None] == cell_block[None, None, :], own_want[:, None, :], -1)
    place = (place == slots[None, :, None]).astype(bf16)
    own_place = lax.dynamic_index_in_dim(place, p, 0, keepdims=False)
    recv, far = lax.optimization_barrier((recv, far))
    recv = recv.reshape(2, groups * peer, 2 * part)
    taken = [jnp.dot(own_place, recv[i], preferred_element_type=f32).astype(bf16) for i in range(2)]
    compact = jnp.concatenate(
        [taken[0][:, :part], taken[1][:, :part], taken[0][:, part:], taken[1][:, part:]], axis=1
    )
    half_cap = capacity // 2
    compact = compact.reshape(2, 1, half_cap, 4 * part)
    spreadout = jnp.broadcast_to(compact, (2, spread, half_cap, 4 * part))
    gathered = lax.all_to_all(
        spreadout.reshape(2 * spread, half_cap, 4 * part),
        ("q", "x", "c"),
        split_axis=0,
        concat_axis=0,
        tiled=True,
    )
    hidden = wg.shape[1]
    width = wg.shape[0]
    weight = lax.dynamic_slice(combine, (p, q * half_cap), (1, half_cap)).reshape(half_cap, 1)
    vmem = pl.BlockSpec(memory_space=pltpu.VMEM)
    held = jax.ShapeDtypeStruct((half_cap, 2 * width + 3 * hidden), bf16)
    piece, keep, give = pl.pallas_call(
        middle,
        out_shape=(
            jax.ShapeDtypeStruct((4 * spread, half_cap // 2 + 16, 2 * part), bf16),
            held,
            held,
        ),
        in_specs=[pl.BlockSpec(memory_space=pltpu.SMEM)] + [vmem] * 2
        + [here] * 4,
        out_specs=(vmem, vmem, vmem),
        scratch_shapes=[
            pltpu.VMEM((2, half_cap, 2 * width), bf16),
            pltpu.VMEM((2,) + wg.shape, bf16),
            pltpu.VMEM((2,) + wu.shape, bf16),
            pltpu.VMEM((2,) + wd.shape, bf16),
            pltpu.SemaphoreType.DMA((5 + width // hidden,)),
        ],
        compiler_params=pltpu.CompilerParams(vmem_limit_bytes=52 * 1024 * 1024),
        cost_estimate=pl.CostEstimate(
            flops=20 * half_cap * width * hidden, bytes_accessed=5 << 20, transcendentals=0
        ),
    )(q.reshape(1), weight, gathered, wg, wu, wd, far)
    pieces = lax.all_to_all(piece, ("p", "q", "x", "c"), split_axis=0, concat_axis=0, tiled=True)
    pieces = pieces.reshape(2, 2, spread, half_cap // 2 + 16, 2 * part)
    summed = jnp.sum(pieces.astype(f32), axis=2)
    term_sum = summed[:, :, half_cap // 2]
    grad_combine = (term_sum[:, :, :half_cap] + term_sum[:, :, half_cap:]).reshape(
        exp_dev, capacity
    )
    summed = summed[:, :, : half_cap // 2].astype(bf16)
    summed = jnp.transpose(
        summed.reshape(exp_dev, 2, half_cap // 2, 2, part), (0, 1, 3, 2, 4)
    ).reshape(exp_dev, capacity, part)

    over_slots = (((0,), (0,)), ((), ()))
    back = jnp.concatenate(
        [
            lax.dot_general(place[i], summed[i], over_slots, preferred_element_type=f32).astype(bf16)
            for i in range(exp_dev)
        ],
        axis=1,
    )
    returned = lax.all_to_all(
        back.reshape(groups, peer, exp_dev * part), "z", split_axis=0, concat_axis=0, tiled=True
    ).reshape(groups * peer, exp_dev * part)
    pick = pick.reshape(exp_dev, groups * peer, tok_dev)
    grad_tokens = lax.dot_general(
        pick[0], returned[:, :part], over_slots, preferred_element_type=f32
    )
    grad_tokens = grad_tokens + lax.dot_general(
        pick[1], returned[:, part:], over_slots, preferred_element_type=f32
    )

    give, _ = lax.optimization_barrier((give, back))
    got = lax.all_gather(give, "q", axis=0)
    got = lax.dynamic_index_in_dim(got, 1 - q, 0, keepdims=False)
    both = jnp.concatenate([keep, got], axis=0)
    rows_in = both[:, :width]
    scaled_out = both[:, width : 2 * width]
    activation = both[:, 2 * width : 2 * width + hidden]
    d_gate = both[:, 2 * width + hidden : 2 * width + 2 * hidden]
    d_up = both[:, 2 * width + 2 * hidden :]
    grad_down = lax.dot_general(activation, scaled_out, over_slots, preferred_element_type=f32)
    grad_gate = lax.dot_general(rows_in, d_gate, over_slots, preferred_element_type=f32)
    grad_up = lax.dot_general(rows_in, d_up, over_slots, preferred_element_type=f32)
    return (
        grad_tokens.astype(bf16),
        grad_gate.astype(bf16)[None],
        grad_up.astype(bf16)[None],
        grad_down.astype(bf16)[None],
        grad_combine,
    )


def solution(mesh):
    groups, lanes = mesh.devices.shape
    split = Mesh(
        mesh.devices.reshape(groups, 2, 2, lanes // 8, 2), ("z", "p", "q", "x", "c")
    )
    mp = ("p", "q", "x", "c")
    placed = (
        P("z", mp),
        P("z", mp),
        P("z", None, mp),
        P("z", None, mp),
        P("z", mp, None),
        P("z", None),
        P(),
    )
    return jax.shard_map(
        local,
        mesh=split,
        in_specs=placed,
        out_specs=(
            P("z", mp),
            P("z", None, mp),
            P("z", None, mp),
            P("z", mp, None),
            P("z", None),
        ),
        check_vma=False,
    )
```

```python
import jax
import jax.numpy as jnp
from jax import lax
from jax.experimental import pallas as pl
from jax.experimental.pallas import tpu as pltpu
from jax.sharding import Mesh
from jax.sharding import PartitionSpec as P


def middle(
    q_ref,
    weight_ref,
    rows_ref,
    wg_own,
    wu_own,
    wd_own,
    far_ref,
    out_ref,
    keep_ref,
    give_ref,
    nat_ref,
    wg_ref,
    wu_ref,
    wd_ref,
    sem,
):
    q = q_ref[0]
    chunk = wg_own.shape[1]
    far = 1 - q
    pairs = [
        [(wg_own, wg_ref.at[q]), (far_ref.at[0], wg_ref.at[far])],
        [(wu_own, wu_ref.at[q]), (far_ref.at[1], wu_ref.at[far])],
        [(wd_own, wd_ref.at[q])]
        + [
            (far_ref.at[2, pl.ds(i * chunk, chunk)], wd_ref.at[far, :, pl.ds(i * chunk, chunk)])
            for i in range(wd_own.shape[1] // chunk)
        ],
    ]
    loads = []
    count = 0
    for group in pairs:
        loads.append([])
        for source, target in group:
            loads[-1].append(pltpu.make_async_copy(source, target, sem.at[count]))
            loads[-1][-1].start()
            count += 1
    bf16 = jnp.bfloat16
    f32 = jnp.float32
    spread = rows_ref.shape[0] // 2
    slots = rows_ref.shape[1]
    width = wg_ref.shape[1]
    hidden = wg_ref.shape[2]
    weight = weight_ref[...]
    low = lax.broadcasted_iota(jnp.int32, (slots, 128), 1) < 64

    def halves(first, second):
        return (
            jnp.where(low[: first.shape[0]], first, pltpu.roll(second, 64, 1)),
            jnp.where(low[: first.shape[0]], pltpu.roll(first, 64, 1), second),
        )

    for side in range(2):
        for kind in range(2):
            for i in range(spread // 2):
                lanes = pl.ds(kind * 128, 128)
                first = rows_ref[side * spread + 2 * i, :, lanes].astype(f32)
                second = rows_ref[side * spread + 2 * i + 1, :, lanes].astype(f32)
                for a, part in enumerate(halves(first, second)):
                    at = kind * width + a * (width // 2) + i * 128
                    nat_ref[side, :, pl.ds(at, 128)] = part.astype(bf16)

    def over(side, kind):
        return nat_ref[side, :, pl.ds(kind * width, width)]

    across = (((1,), (1,)), ((), ()))
    for load in loads[0]:
        load.wait()
    gate_pre = jnp.dot(over(0, 0), wg_ref[0], preferred_element_type=f32)
    gate_pre = gate_pre + jnp.dot(over(1, 0), wg_ref[1], preferred_element_type=f32)
    for load in loads[1]:
        load.wait()
    up_pre = jnp.dot(over(0, 0), wu_ref[0], preferred_element_type=f32)
    up_pre = up_pre + jnp.dot(over(1, 0), wu_ref[1], preferred_element_type=f32)
    for load in loads[2]:
        load.wait()
    back_grad = lax.dot_general(over(0, 1), wd_ref[0], across, preferred_element_type=f32)
    back_grad = back_grad + lax.dot_general(
        over(1, 1), wd_ref[1], across, preferred_element_type=f32
    )
    sig = 1.0 / (1.0 + jnp.exp(-gate_pre))
    activation = (gate_pre * sig * up_pre).astype(bf16)
    term = jnp.sum(activation.astype(f32) * back_grad, axis=1, keepdims=True)
    d_act = weight * back_grad
    d_gate = (d_act * up_pre * sig * (1.0 + gate_pre * (1.0 - sig))).astype(bf16)
    d_up = (d_act * gate_pre * sig).astype(bf16)

    lane = lax.broadcasted_iota(jnp.int32, (slots, 128), 1)
    slot = lax.broadcasted_iota(jnp.int32, (slots, 128), 0)
    line = jnp.sum(jnp.where((lane & 63) == slot, term, 0.0), axis=0, keepdims=True)
    rounded = line.astype(bf16).astype(f32)
    line = jnp.where(low[:1], rounded, line - rounded)
    extra = jnp.where(slot[:16] == 0, line, 0.0).astype(bf16)
    half = slots // 2
    for side in range(2):
        piece = lax.dot_general(d_gate, wg_ref[side], across, preferred_element_type=f32)
        piece = piece + lax.dot_general(d_up, wu_ref[side], across, preferred_element_type=f32)
        for a in range(2):
            for i in range(spread // 2):
                at = a * (width // 2) + i * 128
                top, bottom = piece[:half, at : at + 128], piece[half:, at : at + 128]
                for j, part in enumerate(halves(top, bottom)):
                    to = (side * 2 + a) * spread + 2 * i + j
                    out_ref[to, pl.ds(0, half), :] = part.astype(bf16)
                    out_ref[to, pl.ds(half, 16), :] = extra

    for ref, side in ((keep_ref, q), (give_ref, 1 - q)):
        ref[:, pl.ds(0, width)] = nat_ref[side, :, pl.ds(0, width)]
        rows_out = nat_ref[side, :, pl.ds(width, width)].astype(f32)
        ref[:, pl.ds(width, width)] = (weight * rows_out).astype(bf16)
        ref[:, pl.ds(2 * width, hidden)] = activation
        ref[:, pl.ds(2 * width + hidden, hidden)] = d_gate
        ref[:, pl.ds(2 * width + 2 * hidden, hidden)] = d_up


def pack(wg_ref, wu_ref, wd_ref, out_ref, sem):
    chunk = wg_ref.shape[1]
    pairs = [(wg_ref, out_ref.at[0]), (wu_ref, out_ref.at[1])] + [
        (wd_ref.at[:, pl.ds(i * chunk, chunk)], out_ref.at[2, pl.ds(i * chunk, chunk)])
        for i in range(wd_ref.shape[1] // chunk)
    ]
    copies = [
        pltpu.make_async_copy(source, target, sem.at[i])
        for i, (source, target) in enumerate(pairs)
    ]
    for copy in copies:
        copy.start()
    for copy in copies:
        copy.wait()


def local(x_tokens, cotangent, w_gate, w_up, w_down, combine, indices):
    bf16 = jnp.bfloat16
    f32 = jnp.float32
    groups = lax.axis_size("z")
    spread = lax.axis_size("x") * lax.axis_size("c")
    tok_dev, part = x_tokens.shape
    experts, capacity = indices.shape
    exp_dev = experts // groups
    peer = 2 * capacity // groups
    z = lax.axis_index("z")
    p = lax.axis_index("p")
    q = lax.axis_index("q")
    wg = w_gate[0]
    wu = w_up[0]
    wd = w_down[0]

    table = jnp.concatenate([x_tokens, cotangent], axis=1)
    table = lax.ppermute(table, ("p", "q"), [(0, 0), (1, 2), (2, 1), (3, 3)])

    swap = [(0, 1), (1, 0)]
    here = pl.BlockSpec(memory_space=pltpu.HBM)
    packed = pl.pallas_call(
        pack,
        out_shape=jax.ShapeDtypeStruct((3,) + wg.shape, bf16),
        in_specs=[here] * 3,
        out_specs=pl.BlockSpec(memory_space=pltpu.VMEM),
        scratch_shapes=[pltpu.SemaphoreType.DMA((6,))],
        cost_estimate=pl.CostEstimate(flops=0, bytes_accessed=3 << 20, transcendentals=0),
    )(wg, wu, wd)
    far = lax.ppermute(packed, "q", swap)

    slots = jnp.arange(capacity, dtype=jnp.int32)
    places = jnp.arange(peer, dtype=jnp.int32)
    tokens = jnp.arange(tok_dev, dtype=jnp.int32)
    ordered = jnp.transpose(indices.reshape(groups, exp_dev, capacity), (1, 0, 2)).reshape(
        experts, capacity
    )
    base = z * tok_dev
    start = jnp.sum(((ordered >= 0) & (ordered < base)).astype(jnp.int32), axis=1)
    want = start[:, None] + places[None, :]
    shifted = jnp.where(ordered >= 0, ordered - base + 1, 0)
    chosen = (
        jnp.sum(jnp.where(slots[None, None, :] == want[:, :, None], shifted[:, None, :], 0), axis=2)
        - 1
    )
    pick = (chosen[:, :, None] == tokens[None, None, :]).astype(bf16)
    pick = pick.reshape(experts * peer, tok_dev)
    send = jnp.dot(pick, table, preferred_element_type=f32).astype(bf16)
    recv = lax.all_to_all(
        send.reshape(experts, peer, 2 * part), ("p", "z"), split_axis=0, concat_axis=0, tiled=True
    )

    own = lax.dynamic_slice_in_dim(indices, z * exp_dev, exp_dev, 0)
    cells = jnp.arange(groups * peer, dtype=jnp.int32)
    cell_block = cells // peer
    earlier = (own[:, None, :] >= 0) & (own[:, None, :] < cell_block[None, :, None] * tok_dev)
    own_want = jnp.sum(earlier.astype(jnp.int32), axis=2) + cells % peer
    own_block = jnp.where(own >= 0, own // tok_dev, -1)
    place = jnp.where(own_block[:, :, None] == cell_block[None, None, :], own_want[:, None, :], -1)
    place = (place == slots[None, :, None]).astype(bf16)
    own_place = lax.dynamic_index_in_dim(place, p, 0, keepdims=False)
    recv, far = lax.optimization_barrier((recv, far))
    recv = recv.reshape(2, groups * peer, 2 * part)
    taken = [jnp.dot(own_place, recv[i], preferred_element_type=f32).astype(bf16) for i in range(2)]
    compact = jnp.concatenate(
        [taken[0][:, :part], taken[1][:, :part], taken[0][:, part:], taken[1][:, part:]], axis=1
    )
    half_cap = capacity // 2
    compact = compact.reshape(2, 1, half_cap, 4 * part)
    spreadout = jnp.broadcast_to(compact, (2, spread, half_cap, 4 * part))
    gathered = lax.all_to_all(
        spreadout.reshape(2 * spread, half_cap, 4 * part),
        ("q", "x", "c"),
        split_axis=0,
        concat_axis=0,
        tiled=True,
    )
    hidden = wg.shape[1]
    width = wg.shape[0]
    weight = lax.dynamic_slice(combine, (p, q * half_cap), (1, half_cap)).reshape(half_cap, 1)
    vmem = pl.BlockSpec(memory_space=pltpu.VMEM)
    held = jax.ShapeDtypeStruct((half_cap, 2 * width + 3 * hidden), bf16)
    piece, keep, give = pl.pallas_call(
        middle,
        out_shape=(
            jax.ShapeDtypeStruct((4 * spread, half_cap // 2 + 16, 2 * part), bf16),
            held,
            held,
        ),
        in_specs=[pl.BlockSpec(memory_space=pltpu.SMEM)] + [vmem] * 2
        + [here] * 4,
        out_specs=(vmem, vmem, vmem),
        scratch_shapes=[
            pltpu.VMEM((2, half_cap, 2 * width), bf16),
            pltpu.VMEM((2,) + wg.shape, bf16),
            pltpu.VMEM((2,) + wu.shape, bf16),
            pltpu.VMEM((2,) + wd.shape, bf16),
            pltpu.SemaphoreType.DMA((5 + width // hidden,)),
        ],
        compiler_params=pltpu.CompilerParams(vmem_limit_bytes=52 * 1024 * 1024),
        cost_estimate=pl.CostEstimate(
            flops=20 * half_cap * width * hidden, bytes_accessed=5 << 20, transcendentals=0
        ),
    )(q.reshape(1), weight, gathered, wg, wu, wd, far)
    pieces = lax.all_to_all(piece, ("p", "q", "x", "c"), split_axis=0, concat_axis=0, tiled=True)
    pieces = pieces.reshape(2, 2, spread, half_cap // 2 + 16, 2 * part)
    summed = jnp.sum(pieces.astype(f32), axis=2)
    term_sum = summed[:, :, half_cap // 2]
    grad_combine = (term_sum[:, :, :half_cap] + term_sum[:, :, half_cap:]).reshape(
        exp_dev, capacity
    )
    summed = summed[:, :, : half_cap // 2].astype(bf16)
    summed = jnp.transpose(
        summed.reshape(exp_dev, 2, half_cap // 2, 2, part), (0, 1, 3, 2, 4)
    ).reshape(exp_dev, capacity, part)

    over_slots = (((0,), (0,)), ((), ()))
    back = jnp.concatenate(
        [
            lax.dot_general(place[i], summed[i], over_slots, preferred_element_type=f32).astype(bf16)
            for i in range(exp_dev)
        ],
        axis=1,
    )
    returned = lax.all_to_all(
        back.reshape(groups, peer, exp_dev * part), "z", split_axis=0, concat_axis=0, tiled=True
    ).reshape(groups * peer, exp_dev * part)
    pick = pick.reshape(exp_dev, groups * peer, tok_dev)
    grad_tokens = lax.dot_general(
        pick[0], returned[:, :part], over_slots, preferred_element_type=f32
    )
    grad_tokens = grad_tokens + lax.dot_general(
        pick[1], returned[:, part:], over_slots, preferred_element_type=f32
    )

    give, _ = lax.optimization_barrier((give, back))
    got = lax.all_gather(give, "q", axis=0)
    got = lax.dynamic_index_in_dim(got, 1 - q, 0, keepdims=False)
    both = jnp.concatenate([keep, got], axis=0)
    rows_in = both[:, :width]
    scaled_out = both[:, width : 2 * width]
    activation = both[:, 2 * width : 2 * width + hidden]
    d_gate = both[:, 2 * width + hidden : 2 * width + 2 * hidden]
    d_up = both[:, 2 * width + 2 * hidden :]
    grad_down = lax.dot_general(activation, scaled_out, over_slots, preferred_element_type=f32)
    grad_gate = lax.dot_general(rows_in, d_gate, over_slots, preferred_element_type=f32)
    grad_up = lax.dot_general(rows_in, d_up, over_slots, preferred_element_type=f32)
    return (
        grad_tokens.astype(bf16),
        grad_gate.astype(bf16)[None],
        grad_up.astype(bf16)[None],
        grad_down.astype(bf16)[None],
        grad_combine,
    )


def solution(mesh):
    groups, lanes = mesh.devices.shape
    split = Mesh(
        mesh.devices.reshape(groups, 2, 2, lanes // 8, 2), ("z", "p", "q", "x", "c")
    )
    mp = ("p", "q", "x", "c")
    placed = (
        P("z", mp),
        P("z", mp),
        P("z", None, mp),
        P("z", None, mp),
        P("z", mp, None),
        P("z", None),
        P(),
    )
    return jax.shard_map(
        local,
        mesh=split,
        in_specs=placed,
        out_specs=(
            P("z", mp),
            P("z", None, mp),
            P("z", None, mp),
            P("z", mp, None),
            P("z", None),
        ),
        check_vma=False,
    )
```

```python
import jax
import jax.numpy as jnp
from jax import lax
from jax.experimental import pallas as pl
from jax.experimental.pallas import tpu as pltpu
from jax.sharding import Mesh
from jax.sharding import PartitionSpec as P


def middle(
    q_ref,
    weight_ref,
    rows_ref,
    wg_own,
    wu_own,
    wd_own,
    far_ref,
    out_ref,
    keep_ref,
    give_ref,
    nat_ref,
    wg_ref,
    wu_ref,
    wd_ref,
    sem,
):
    q = q_ref[0]
    chunk = wg_own.shape[1]
    far = 1 - q
    pairs = [
        [(wg_own, wg_ref.at[q]), (far_ref.at[0], wg_ref.at[far])],
        [(wu_own, wu_ref.at[q]), (far_ref.at[1], wu_ref.at[far])],
        [(wd_own, wd_ref.at[q])]
        + [
            (far_ref.at[2, pl.ds(i * chunk, chunk)], wd_ref.at[far, :, pl.ds(i * chunk, chunk)])
            for i in range(wd_own.shape[1] // chunk)
        ],
    ]
    loads = []
    count = 0
    for group in pairs:
        loads.append([])
        for source, target in group:
            loads[-1].append(pltpu.make_async_copy(source, target, sem.at[count]))
            loads[-1][-1].start()
            count += 1
    bf16 = jnp.bfloat16
    f32 = jnp.float32
    spread = rows_ref.shape[0] // 2
    slots = rows_ref.shape[1]
    width = wg_ref.shape[1]
    hidden = wg_ref.shape[2]
    weight = weight_ref[...]
    low = lax.broadcasted_iota(jnp.int32, (slots, 128), 1) < 64

    def halves(first, second):
        return (
            jnp.where(low[: first.shape[0]], first, pltpu.roll(second, 64, 1)),
            jnp.where(low[: first.shape[0]], pltpu.roll(first, 64, 1), second),
        )

    for side in range(2):
        for kind in range(2):
            for i in range(spread // 2):
                lanes = pl.ds(kind * 128, 128)
                first = rows_ref[side * spread + 2 * i, :, lanes].astype(f32)
                second = rows_ref[side * spread + 2 * i + 1, :, lanes].astype(f32)
                for a, part in enumerate(halves(first, second)):
                    at = kind * width + a * (width // 2) + i * 128
                    nat_ref[side, :, pl.ds(at, 128)] = part.astype(bf16)

    def over(side, kind):
        return nat_ref[side, :, pl.ds(kind * width, width)]

    across = (((1,), (1,)), ((), ()))
    for load in loads[0]:
        load.wait()
    gate_pre = jnp.dot(over(0, 0), wg_ref[0], preferred_element_type=f32)
    gate_pre = gate_pre + jnp.dot(over(1, 0), wg_ref[1], preferred_element_type=f32)
    for load in loads[1]:
        load.wait()
    up_pre = jnp.dot(over(0, 0), wu_ref[0], preferred_element_type=f32)
    up_pre = up_pre + jnp.dot(over(1, 0), wu_ref[1], preferred_element_type=f32)
    for load in loads[2]:
        load.wait()
    back_grad = lax.dot_general(over(0, 1), wd_ref[0], across, preferred_element_type=f32)
    back_grad = back_grad + lax.dot_general(
        over(1, 1), wd_ref[1], across, preferred_element_type=f32
    )
    sig = 1.0 / (1.0 + jnp.exp(-gate_pre))
    activation = (gate_pre * sig * up_pre).astype(bf16)
    term = jnp.sum(activation.astype(f32) * back_grad, axis=1, keepdims=True)
    d_act = weight * back_grad
    d_gate = (d_act * up_pre * sig * (1.0 + gate_pre * (1.0 - sig))).astype(bf16)
    d_up = (d_act * gate_pre * sig).astype(bf16)

    lane = lax.broadcasted_iota(jnp.int32, (slots, 128), 1)
    slot = lax.broadcasted_iota(jnp.int32, (slots, 128), 0)
    line = jnp.sum(jnp.where((lane & 63) == slot, term, 0.0), axis=0, keepdims=True)
    rounded = line.astype(bf16).astype(f32)
    line = jnp.where(low[:1], rounded, line - rounded)
    extra = jnp.where(slot[:16] == 0, line, 0.0).astype(bf16)
    half = slots // 2
    for side in range(2):
        piece = lax.dot_general(d_gate, wg_ref[side], across, preferred_element_type=f32)
        piece = piece + lax.dot_general(d_up, wu_ref[side], across, preferred_element_type=f32)
        for a in range(2):
            for i in range(spread // 2):
                at = a * (width // 2) + i * 128
                top, bottom = piece[:half, at : at + 128], piece[half:, at : at + 128]
                for j, part in enumerate(halves(top, bottom)):
                    to = (side * 2 + a) * spread + 2 * i + j
                    out_ref[to, pl.ds(0, half), :] = part.astype(bf16)
                    out_ref[to, pl.ds(half, 16), :] = extra

    for ref, side in ((keep_ref, q), (give_ref, 1 - q)):
        ref[:, pl.ds(0, width)] = nat_ref[side, :, pl.ds(0, width)]
        rows_out = nat_ref[side, :, pl.ds(width, width)].astype(f32)
        ref[:, pl.ds(width, width)] = (weight * rows_out).astype(bf16)
        ref[:, pl.ds(2 * width, hidden)] = activation
        ref[:, pl.ds(2 * width + hidden, hidden)] = d_gate
        ref[:, pl.ds(2 * width + 2 * hidden, hidden)] = d_up


def pack(wg_ref, wu_ref, wd_ref, out_ref, sem):
    chunk = wg_ref.shape[1]
    pairs = [(wg_ref, out_ref.at[0]), (wu_ref, out_ref.at[1])] + [
        (wd_ref.at[:, pl.ds(i * chunk, chunk)], out_ref.at[2, pl.ds(i * chunk, chunk)])
        for i in range(wd_ref.shape[1] // chunk)
    ]
    copies = [
        pltpu.make_async_copy(source, target, sem.at[i])
        for i, (source, target) in enumerate(pairs)
    ]
    for copy in copies:
        copy.start()
    for copy in copies:
        copy.wait()


def local(x_tokens, cotangent, w_gate, w_up, w_down, combine, indices):
    bf16 = jnp.bfloat16
    f32 = jnp.float32
    groups = lax.axis_size("z")
    spread = lax.axis_size("x") * lax.axis_size("c")
    tok_dev, part = x_tokens.shape
    experts, capacity = indices.shape
    exp_dev = experts // groups
    peer = 2 * capacity // groups
    z = lax.axis_index("z")
    p = lax.axis_index("p")
    q = lax.axis_index("q")
    wg = w_gate[0]
    wu = w_up[0]
    wd = w_down[0]

    table = jnp.concatenate([x_tokens, cotangent], axis=1)
    table = lax.ppermute(table, ("p", "q"), [(0, 0), (1, 2), (2, 1), (3, 3)])

    slots = jnp.arange(capacity, dtype=jnp.int32)
    places = jnp.arange(peer, dtype=jnp.int32)
    tokens = jnp.arange(tok_dev, dtype=jnp.int32)
    ordered = jnp.transpose(indices.reshape(groups, exp_dev, capacity), (1, 0, 2)).reshape(
        experts, capacity
    )
    base = z * tok_dev
    start = jnp.sum(((ordered >= 0) & (ordered < base)).astype(jnp.int32), axis=1)
    want = start[:, None] + places[None, :]
    shifted = jnp.where(ordered >= 0, ordered - base + 1, 0)
    chosen = (
        jnp.sum(jnp.where(slots[None, None, :] == want[:, :, None], shifted[:, None, :], 0), axis=2)
        - 1
    )
    pick = (chosen[:, :, None] == tokens[None, None, :]).astype(bf16)
    pick = pick.reshape(experts * peer, tok_dev)
    send = jnp.dot(pick, table, preferred_element_type=f32).astype(bf16)
    send, *give_weights = lax.optimization_barrier((send, wg, wu, wd))
    swap = [(0, 1), (1, 0)]
    here = pl.BlockSpec(memory_space=pltpu.HBM)
    packed = pl.pallas_call(
        pack,
        out_shape=jax.ShapeDtypeStruct((3,) + wg.shape, bf16),
        in_specs=[here] * 3,
        out_specs=pl.BlockSpec(memory_space=pltpu.VMEM),
        scratch_shapes=[pltpu.SemaphoreType.DMA((6,))],
        cost_estimate=pl.CostEstimate(flops=0, bytes_accessed=3 << 20, transcendentals=0),
    )(*give_weights)
    far = lax.ppermute(packed, "q", swap)
    recv = lax.all_to_all(
        send.reshape(experts, peer, 2 * part), ("p", "z"), split_axis=0, concat_axis=0, tiled=True
    )

    own = lax.dynamic_slice_in_dim(indices, z * exp_dev, exp_dev, 0)
    cells = jnp.arange(groups * peer, dtype=jnp.int32)
    cell_block = cells // peer
    earlier = (own[:, None, :] >= 0) & (own[:, None, :] < cell_block[None, :, None] * tok_dev)
    own_want = jnp.sum(earlier.astype(jnp.int32), axis=2) + cells % peer
    own_block = jnp.where(own >= 0, own // tok_dev, -1)
    place = jnp.where(own_block[:, :, None] == cell_block[None, None, :], own_want[:, None, :], -1)
    place = (place == slots[None, :, None]).astype(bf16)
    own_place = lax.dynamic_index_in_dim(place, p, 0, keepdims=False)
    recv = recv.reshape(2, groups * peer, 2 * part)
    taken = [jnp.dot(own_place, recv[i], preferred_element_type=f32).astype(bf16) for i in range(2)]
    compact = jnp.concatenate(
        [taken[0][:, :part], taken[1][:, :part], taken[0][:, part:], taken[1][:, part:]], axis=1
    )
    half_cap = capacity // 2
    compact = compact.reshape(2, 1, half_cap, 4 * part)
    spreadout = jnp.broadcast_to(compact, (2, spread, half_cap, 4 * part))
    gathered = lax.all_to_all(
        spreadout.reshape(2 * spread, half_cap, 4 * part),
        ("q", "x", "c"),
        split_axis=0,
        concat_axis=0,
        tiled=True,
    )
    hidden = wg.shape[1]
    width = wg.shape[0]
    weight = lax.dynamic_slice(combine, (p, q * half_cap), (1, half_cap)).reshape(half_cap, 1)
    vmem = pl.BlockSpec(memory_space=pltpu.VMEM)
    held = jax.ShapeDtypeStruct((half_cap, 2 * width + 3 * hidden), bf16)
    piece, keep, give = pl.pallas_call(
        middle,
        out_shape=(
            jax.ShapeDtypeStruct((4 * spread, half_cap // 2 + 16, 2 * part), bf16),
            held,
            held,
        ),
        in_specs=[pl.BlockSpec(memory_space=pltpu.SMEM)] + [vmem] * 2
        + [pl.BlockSpec(memory_space=pl.ANY)] * 4,
        out_specs=(vmem, vmem, vmem),
        scratch_shapes=[
            pltpu.VMEM((2, half_cap, 2 * width), bf16),
            pltpu.VMEM((2,) + wg.shape, bf16),
            pltpu.VMEM((2,) + wu.shape, bf16),
            pltpu.VMEM((2,) + wd.shape, bf16),
            pltpu.SemaphoreType.DMA((5 + width // hidden,)),
        ],
        compiler_params=pltpu.CompilerParams(vmem_limit_bytes=40 * 1024 * 1024),
        cost_estimate=pl.CostEstimate(
            flops=20 * half_cap * width * hidden, bytes_accessed=5 << 20, transcendentals=0
        ),
    )(q.reshape(1), weight, gathered, wg, wu, wd, far)
    pieces = lax.all_to_all(piece, ("p", "q", "x", "c"), split_axis=0, concat_axis=0, tiled=True)
    pieces = pieces.reshape(2, 2, spread, half_cap // 2 + 16, 2 * part)
    summed = jnp.sum(pieces.astype(f32), axis=2)
    term_sum = summed[:, :, half_cap // 2]
    grad_combine = (term_sum[:, :, :half_cap] + term_sum[:, :, half_cap:]).reshape(
        exp_dev, capacity
    )
    summed = summed[:, :, : half_cap // 2].astype(bf16)
    summed = jnp.transpose(
        summed.reshape(exp_dev, 2, half_cap // 2, 2, part), (0, 1, 3, 2, 4)
    ).reshape(exp_dev, capacity, part)

    over_slots = (((0,), (0,)), ((), ()))
    back = jnp.concatenate(
        [
            lax.dot_general(place[i], summed[i], over_slots, preferred_element_type=f32).astype(bf16)
            for i in range(exp_dev)
        ],
        axis=1,
    )
    returned = lax.all_to_all(
        back.reshape(groups, peer, exp_dev * part), "z", split_axis=0, concat_axis=0, tiled=True
    ).reshape(groups * peer, exp_dev * part)
    pick = pick.reshape(exp_dev, groups * peer, tok_dev)
    grad_tokens = lax.dot_general(
        pick[0], returned[:, :part], over_slots, preferred_element_type=f32
    )
    grad_tokens = grad_tokens + lax.dot_general(
        pick[1], returned[:, part:], over_slots, preferred_element_type=f32
    )

    give, _ = lax.optimization_barrier((give, back))
    got = lax.all_gather(give, "q", axis=0)
    got = lax.dynamic_index_in_dim(got, 1 - q, 0, keepdims=False)
    both = jnp.concatenate([keep, got], axis=0)
    rows_in = both[:, :width]
    scaled_out = both[:, width : 2 * width]
    activation = both[:, 2 * width : 2 * width + hidden]
    d_gate = both[:, 2 * width + hidden : 2 * width + 2 * hidden]
    d_up = both[:, 2 * width + 2 * hidden :]
    grad_down = lax.dot_general(activation, scaled_out, over_slots, preferred_element_type=f32)
    grad_gate = lax.dot_general(rows_in, d_gate, over_slots, preferred_element_type=f32)
    grad_up = lax.dot_general(rows_in, d_up, over_slots, preferred_element_type=f32)
    return (
        grad_tokens.astype(bf16),
        grad_gate.astype(bf16)[None],
        grad_up.astype(bf16)[None],
        grad_down.astype(bf16)[None],
        grad_combine,
    )


def solution(mesh):
    groups, lanes = mesh.devices.shape
    split = Mesh(
        mesh.devices.reshape(groups, 2, 2, lanes // 8, 2), ("z", "p", "q", "x", "c")
    )
    mp = ("p", "q", "x", "c")
    placed = (
        P("z", mp),
        P("z", mp),
        P("z", None, mp),
        P("z", None, mp),
        P("z", mp, None),
        P("z", None),
        P(),
    )
    return jax.shard_map(
        local,
        mesh=split,
        in_specs=placed,
        out_specs=(
            P("z", mp),
            P("z", None, mp),
            P("z", None, mp),
            P("z", mp, None),
            P("z", None),
        ),
        check_vma=False,
    )
```

```python
import jax
import jax.numpy as jnp
from jax import lax
from jax.experimental import pallas as pl
from jax.experimental.pallas import tpu as pltpu
from jax.sharding import Mesh
from jax.sharding import PartitionSpec as P


def middle(
    q_ref,
    weight_ref,
    rows_ref,
    wg_own,
    wu_own,
    wd_own,
    far_ref,
    out_ref,
    keep_ref,
    give_ref,
    nat_ref,
    wg_ref,
    wu_ref,
    wd_ref,
    sem,
):
    q = q_ref[0]
    chunk = wg_own.shape[1]
    far = 1 - q
    pairs = [
        [(wg_own, wg_ref.at[q]), (far_ref.at[0], wg_ref.at[far])],
        [(wu_own, wu_ref.at[q]), (far_ref.at[1], wu_ref.at[far])],
        [(wd_own, wd_ref.at[q])]
        + [
            (far_ref.at[2, pl.ds(i * chunk, chunk)], wd_ref.at[far, :, pl.ds(i * chunk, chunk)])
            for i in range(wd_own.shape[1] // chunk)
        ],
    ]
    loads = []
    count = 0
    for group in pairs:
        loads.append([])
        for source, target in group:
            loads[-1].append(pltpu.make_async_copy(source, target, sem.at[count]))
            loads[-1][-1].start()
            count += 1
    bf16 = jnp.bfloat16
    f32 = jnp.float32
    spread = rows_ref.shape[0] // 2
    slots = rows_ref.shape[1]
    width = wg_ref.shape[1]
    hidden = wg_ref.shape[2]
    weight = weight_ref[...]
    low = lax.broadcasted_iota(jnp.int32, (slots, 128), 1) < 64

    def halves(first, second):
        return (
            jnp.where(low[: first.shape[0]], first, pltpu.roll(second, 64, 1)),
            jnp.where(low[: first.shape[0]], pltpu.roll(first, 64, 1), second),
        )

    for side in range(2):
        for kind in range(2):
            for i in range(spread // 2):
                lanes = pl.ds(kind * 128, 128)
                first = rows_ref[side * spread + 2 * i, :, lanes].astype(f32)
                second = rows_ref[side * spread + 2 * i + 1, :, lanes].astype(f32)
                for a, part in enumerate(halves(first, second)):
                    at = kind * width + a * (width // 2) + i * 128
                    nat_ref[side, :, pl.ds(at, 128)] = part.astype(bf16)

    def over(side, kind):
        return nat_ref[side, :, pl.ds(kind * width, width)]

    across = (((1,), (1,)), ((), ()))
    for load in loads[0]:
        load.wait()
    gate_pre = jnp.dot(over(0, 0), wg_ref[0], preferred_element_type=f32)
    gate_pre = gate_pre + jnp.dot(over(1, 0), wg_ref[1], preferred_element_type=f32)
    for load in loads[1]:
        load.wait()
    up_pre = jnp.dot(over(0, 0), wu_ref[0], preferred_element_type=f32)
    up_pre = up_pre + jnp.dot(over(1, 0), wu_ref[1], preferred_element_type=f32)
    for load in loads[2]:
        load.wait()
    back_grad = lax.dot_general(over(0, 1), wd_ref[0], across, preferred_element_type=f32)
    back_grad = back_grad + lax.dot_general(
        over(1, 1), wd_ref[1], across, preferred_element_type=f32
    )
    sig = 1.0 / (1.0 + jnp.exp(-gate_pre))
    activation = (gate_pre * sig * up_pre).astype(bf16)
    term = jnp.sum(activation.astype(f32) * back_grad, axis=1, keepdims=True)
    d_act = weight * back_grad
    d_gate = (d_act * up_pre * sig * (1.0 + gate_pre * (1.0 - sig))).astype(bf16)
    d_up = (d_act * gate_pre * sig).astype(bf16)

    lane = lax.broadcasted_iota(jnp.int32, (slots, 128), 1)
    slot = lax.broadcasted_iota(jnp.int32, (slots, 128), 0)
    line = jnp.sum(jnp.where((lane & 63) == slot, term, 0.0), axis=0, keepdims=True)
    rounded = line.astype(bf16).astype(f32)
    line = jnp.where(low[:1], rounded, line - rounded)
    extra = jnp.where(slot[:16] == 0, line, 0.0).astype(bf16)
    half = slots // 2
    for side in range(2):
        piece = lax.dot_general(d_gate, wg_ref[side], across, preferred_element_type=f32)
        piece = piece + lax.dot_general(d_up, wu_ref[side], across, preferred_element_type=f32)
        for a in range(2):
            for i in range(spread // 2):
                at = a * (width // 2) + i * 128
                top, bottom = piece[:half, at : at + 128], piece[half:, at : at + 128]
                for j, part in enumerate(halves(top, bottom)):
                    to = (side * 2 + a) * spread + 2 * i + j
                    out_ref[to, pl.ds(0, half), :] = part.astype(bf16)
                    out_ref[to, pl.ds(half, 16), :] = extra

    for ref, side in ((keep_ref, q), (give_ref, 1 - q)):
        ref[:, pl.ds(0, width)] = nat_ref[side, :, pl.ds(0, width)]
        rows_out = nat_ref[side, :, pl.ds(width, width)].astype(f32)
        ref[:, pl.ds(width, width)] = (weight * rows_out).astype(bf16)
        ref[:, pl.ds(2 * width, hidden)] = activation
        ref[:, pl.ds(2 * width + hidden, hidden)] = d_gate
        ref[:, pl.ds(2 * width + 2 * hidden, hidden)] = d_up


def prepare(base_ref, indices_ref, wg_ref, wu_ref, wd_ref, out_ref, pick_ref, sem):
    chunk = wg_ref.shape[1]
    pairs = [(wg_ref, out_ref.at[0]), (wu_ref, out_ref.at[1])] + [
        (wd_ref.at[:, pl.ds(i * chunk, chunk)], out_ref.at[2, pl.ds(i * chunk, chunk)])
        for i in range(wd_ref.shape[1] // chunk)
    ]
    copies = [
        pltpu.make_async_copy(source, target, sem.at[i])
        for i, (source, target) in enumerate(pairs)
    ]
    for copy in copies:
        copy.start()
    f32 = jnp.float32
    experts, capacity = indices_ref.shape
    groups = experts // 2
    peer = pick_ref.shape[0] // experts
    base = base_ref[0]
    lane = lax.broadcasted_iota(jnp.int32, (groups, capacity), 1).astype(f32)
    for member in range(2):
        tokens = indices_ref[pl.ds(member, groups, stride=2), :]
        live = tokens >= 0
        before = jnp.where(live & (tokens < base), 1.0, 0.0)
        start = jnp.sum(before, axis=1, keepdims=True)
        shifted = jnp.where(live, tokens - base + 1, 0).astype(f32)
        for place in range(peer):
            at_place = jnp.where(lane == start + place, shifted, 0.0)
            chosen = jnp.sum(at_place, axis=1, keepdims=True) - 1.0
            rows = pl.ds(member * groups * peer + place, groups, stride=peer)
            pick_ref[rows, :] = jnp.where(lane == chosen, 1.0, 0.0)
    for copy in copies:
        copy.wait()


def local(x_tokens, cotangent, w_gate, w_up, w_down, combine, indices):
    bf16 = jnp.bfloat16
    f32 = jnp.float32
    groups = lax.axis_size("z")
    spread = lax.axis_size("x") * lax.axis_size("c")
    tok_dev, part = x_tokens.shape
    experts, capacity = indices.shape
    exp_dev = experts // groups
    peer = 2 * capacity // groups
    z = lax.axis_index("z")
    p = lax.axis_index("p")
    q = lax.axis_index("q")
    wg = w_gate[0]
    wu = w_up[0]
    wd = w_down[0]

    table = jnp.concatenate([x_tokens, cotangent], axis=1)
    table = lax.ppermute(table, ("p", "q"), [(0, 0), (1, 2), (2, 1), (3, 3)])

    swap = [(0, 1), (1, 0)]
    here = pl.BlockSpec(memory_space=pltpu.HBM)
    whole = pl.BlockSpec(memory_space=pltpu.VMEM)
    packed, pick = pl.pallas_call(
        prepare,
        out_shape=(
            jax.ShapeDtypeStruct((3,) + wg.shape, bf16),
            jax.ShapeDtypeStruct((experts * peer, tok_dev), f32),
        ),
        in_specs=[pl.BlockSpec(memory_space=pltpu.SMEM), whole] + [here] * 3,
        out_specs=(whole, whole),
        scratch_shapes=[pltpu.SemaphoreType.DMA((6,))],
        cost_estimate=pl.CostEstimate(flops=0, bytes_accessed=3 << 20, transcendentals=0),
    )((z * tok_dev).reshape(1), indices, wg, wu, wd)
    pick = pick.astype(bf16)
    packed, table = lax.optimization_barrier((packed, table))
    far = lax.ppermute(packed, "q", swap)

    slots = jnp.arange(capacity, dtype=jnp.int32)
    send = jnp.dot(pick, table, preferred_element_type=f32).astype(bf16)
    recv = lax.all_to_all(
        send.reshape(experts, peer, 2 * part), ("p", "z"), split_axis=0, concat_axis=0, tiled=True
    )

    own = lax.dynamic_slice_in_dim(indices, z * exp_dev, exp_dev, 0)
    cells = jnp.arange(groups * peer, dtype=jnp.int32)
    cell_block = cells // peer
    earlier = (own[:, None, :] >= 0) & (own[:, None, :] < cell_block[None, :, None] * tok_dev)
    own_want = jnp.sum(earlier.astype(jnp.int32), axis=2) + cells % peer
    own_block = jnp.where(own >= 0, own // tok_dev, -1)
    place = jnp.where(own_block[:, :, None] == cell_block[None, None, :], own_want[:, None, :], -1)
    place = (place == slots[None, :, None]).astype(bf16)
    own_place = lax.dynamic_index_in_dim(place, p, 0, keepdims=False)
    recv, far = lax.optimization_barrier((recv, far))
    recv = recv.reshape(2, groups * peer, 2 * part)
    taken = [jnp.dot(own_place, recv[i], preferred_element_type=f32).astype(bf16) for i in range(2)]
    compact = jnp.concatenate(
        [taken[0][:, :part], taken[1][:, :part], taken[0][:, part:], taken[1][:, part:]], axis=1
    )
    half_cap = capacity // 2
    compact = compact.reshape(2, 1, half_cap, 4 * part)
    spreadout = jnp.broadcast_to(compact, (2, spread, half_cap, 4 * part))
    gathered = lax.all_to_all(
        spreadout.reshape(2 * spread, half_cap, 4 * part),
        ("q", "x", "c"),
        split_axis=0,
        concat_axis=0,
        tiled=True,
    )
    hidden = wg.shape[1]
    width = wg.shape[0]
    weight = lax.dynamic_slice(combine, (p, q * half_cap), (1, half_cap)).reshape(half_cap, 1)
    vmem = pl.BlockSpec(memory_space=pltpu.VMEM)
    held = jax.ShapeDtypeStruct((half_cap, 2 * width + 3 * hidden), bf16)
    piece, keep, give = pl.pallas_call(
        middle,
        out_shape=(
            jax.ShapeDtypeStruct((4 * spread, half_cap // 2 + 16, 2 * part), bf16),
            held,
            held,
        ),
        in_specs=[pl.BlockSpec(memory_space=pltpu.SMEM)] + [vmem] * 2
        + [here] * 4,
        out_specs=(vmem, vmem, vmem),
        scratch_shapes=[
            pltpu.VMEM((2, half_cap, 2 * width), bf16),
            pltpu.VMEM((2,) + wg.shape, bf16),
            pltpu.VMEM((2,) + wu.shape, bf16),
            pltpu.VMEM((2,) + wd.shape, bf16),
            pltpu.SemaphoreType.DMA((5 + width // hidden,)),
        ],
        compiler_params=pltpu.CompilerParams(vmem_limit_bytes=52 * 1024 * 1024),
        cost_estimate=pl.CostEstimate(
            flops=20 * half_cap * width * hidden, bytes_accessed=5 << 20, transcendentals=0
        ),
    )(q.reshape(1), weight, gathered, wg, wu, wd, far)
    pieces = lax.all_to_all(piece, ("p", "q", "x", "c"), split_axis=0, concat_axis=0, tiled=True)
    pieces = pieces.reshape(2, 2, spread, half_cap // 2 + 16, 2 * part)
    summed = jnp.sum(pieces.astype(f32), axis=2)
    term_sum = summed[:, :, half_cap // 2]
    grad_combine = (term_sum[:, :, :half_cap] + term_sum[:, :, half_cap:]).reshape(
        exp_dev, capacity
    )
    summed = summed[:, :, : half_cap // 2].astype(bf16)
    summed = jnp.transpose(
        summed.reshape(exp_dev, 2, half_cap // 2, 2, part), (0, 1, 3, 2, 4)
    ).reshape(exp_dev, capacity, part)

    over_slots = (((0,), (0,)), ((), ()))
    back = jnp.concatenate(
        [
            lax.dot_general(place[i], summed[i], over_slots, preferred_element_type=f32).astype(bf16)
            for i in range(exp_dev)
        ],
        axis=1,
    )
    returned = lax.all_to_all(
        back.reshape(groups, peer, exp_dev * part), "z", split_axis=0, concat_axis=0, tiled=True
    ).reshape(groups * peer, exp_dev * part)
    pick = pick.reshape(exp_dev, groups * peer, tok_dev)
    grad_tokens = lax.dot_general(
        pick[0], returned[:, :part], over_slots, preferred_element_type=f32
    )
    grad_tokens = grad_tokens + lax.dot_general(
        pick[1], returned[:, part:], over_slots, preferred_element_type=f32
    )

    give, _ = lax.optimization_barrier((give, back))
    got = lax.all_gather(give, "q", axis=0)
    got = lax.dynamic_index_in_dim(got, 1 - q, 0, keepdims=False)
    both = jnp.concatenate([keep, got], axis=0)
    rows_in = both[:, :width]
    scaled_out = both[:, width : 2 * width]
    activation = both[:, 2 * width : 2 * width + hidden]
    d_gate = both[:, 2 * width + hidden : 2 * width + 2 * hidden]
    d_up = both[:, 2 * width + 2 * hidden :]
    grad_down = lax.dot_general(activation, scaled_out, over_slots, preferred_element_type=f32)
    grad_gate = lax.dot_general(rows_in, d_gate, over_slots, preferred_element_type=f32)
    grad_up = lax.dot_general(rows_in, d_up, over_slots, preferred_element_type=f32)
    return (
        grad_tokens.astype(bf16),
        grad_gate.astype(bf16)[None],
        grad_up.astype(bf16)[None],
        grad_down.astype(bf16)[None],
        grad_combine,
    )


def solution(mesh):
    groups, lanes = mesh.devices.shape
    split = Mesh(
        mesh.devices.reshape(groups, 2, 2, lanes // 8, 2), ("z", "p", "q", "x", "c")
    )
    mp = ("p", "q", "x", "c")
    placed = (
        P("z", mp),
        P("z", mp),
        P("z", None, mp),
        P("z", None, mp),
        P("z", mp, None),
        P("z", None),
        P(),
    )
    return jax.shard_map(
        local,
        mesh=split,
        in_specs=placed,
        out_specs=(
            P("z", mp),
            P("z", None, mp),
            P("z", None, mp),
            P("z", mp, None),
            P("z", None),
        ),
        check_vma=False,
    )
```

```python
import jax
import jax.numpy as jnp
from jax import lax
from jax.experimental import pallas as pl
from jax.experimental.pallas import tpu as pltpu
from jax.sharding import Mesh
from jax.sharding import PartitionSpec as P


def middle(
    q_ref,
    weight_ref,
    rows_ref,
    wg_own,
    wu_own,
    wd_own,
    far_ref,
    out_ref,
    keep_ref,
    give_ref,
    nat_ref,
    wg_ref,
    wu_ref,
    wd_ref,
    sem,
):
    q = q_ref[0]
    chunk = wg_own.shape[1]
    far = 1 - q
    pairs = [
        [(wg_own, wg_ref.at[q]), (far_ref.at[0], wg_ref.at[far])],
        [(wu_own, wu_ref.at[q]), (far_ref.at[1], wu_ref.at[far])],
        [(wd_own, wd_ref.at[q])]
        + [
            (far_ref.at[2, pl.ds(i * chunk, chunk)], wd_ref.at[far, :, pl.ds(i * chunk, chunk)])
            for i in range(wd_own.shape[1] // chunk)
        ],
    ]
    loads = []
    count = 0
    for group in pairs:
        loads.append([])
        for source, target in group:
            loads[-1].append(pltpu.make_async_copy(source, target, sem.at[count]))
            loads[-1][-1].start()
            count += 1
    bf16 = jnp.bfloat16
    f32 = jnp.float32
    spread = rows_ref.shape[0] // 2
    slots = rows_ref.shape[1]
    width = wg_ref.shape[1]
    hidden = wg_ref.shape[2]
    weight = weight_ref[...]
    low = lax.broadcasted_iota(jnp.int32, (slots, 128), 1) < 64

    def halves(first, second):
        return (
            jnp.where(low[: first.shape[0]], first, pltpu.roll(second, 64, 1)),
            jnp.where(low[: first.shape[0]], pltpu.roll(first, 64, 1), second),
        )

    for side in range(2):
        for kind in range(2):
            for i in range(spread // 2):
                lanes = pl.ds(kind * 128, 128)
                first = rows_ref[side * spread + 2 * i, :, lanes].astype(f32)
                second = rows_ref[side * spread + 2 * i + 1, :, lanes].astype(f32)
                for a, part in enumerate(halves(first, second)):
                    at = kind * width + a * (width // 2) + i * 128
                    nat_ref[side, :, pl.ds(at, 128)] = part.astype(bf16)

    def over(side, kind):
        return nat_ref[side, :, pl.ds(kind * width, width)]

    across = (((1,), (1,)), ((), ()))
    for load in loads[0]:
        load.wait()
    gate_pre = jnp.dot(over(0, 0), wg_ref[0], preferred_element_type=f32)
    gate_pre = gate_pre + jnp.dot(over(1, 0), wg_ref[1], preferred_element_type=f32)
    for load in loads[1]:
        load.wait()
    up_pre = jnp.dot(over(0, 0), wu_ref[0], preferred_element_type=f32)
    up_pre = up_pre + jnp.dot(over(1, 0), wu_ref[1], preferred_element_type=f32)
    for load in loads[2]:
        load.wait()
    back_grad = lax.dot_general(over(0, 1), wd_ref[0], across, preferred_element_type=f32)
    back_grad = back_grad + lax.dot_general(
        over(1, 1), wd_ref[1], across, preferred_element_type=f32
    )
    sig = 1.0 / (1.0 + jnp.exp(-gate_pre))
    activation = (gate_pre * sig * up_pre).astype(bf16)
    term = jnp.sum(activation.astype(f32) * back_grad, axis=1, keepdims=True)
    d_act = weight * back_grad
    d_gate = (d_act * up_pre * sig * (1.0 + gate_pre * (1.0 - sig))).astype(bf16)
    d_up = (d_act * gate_pre * sig).astype(bf16)

    lane = lax.broadcasted_iota(jnp.int32, (slots, 128), 1)
    slot = lax.broadcasted_iota(jnp.int32, (slots, 128), 0)
    line = jnp.sum(jnp.where((lane & 63) == slot, term, 0.0), axis=0, keepdims=True)
    rounded = line.astype(bf16).astype(f32)
    line = jnp.where(low[:1], rounded, line - rounded)
    extra = jnp.where(slot[:16] == 0, line, 0.0).astype(bf16)
    half = slots // 2
    for side in range(2):
        piece = lax.dot_general(d_gate, wg_ref[side], across, preferred_element_type=f32)
        piece = piece + lax.dot_general(d_up, wu_ref[side], across, preferred_element_type=f32)
        for a in range(2):
            for i in range(spread // 2):
                at = a * (width // 2) + i * 128
                top, bottom = piece[:half, at : at + 128], piece[half:, at : at + 128]
                for j, part in enumerate(halves(top, bottom)):
                    to = (side * 2 + a) * spread + 2 * i + j
                    out_ref[to, pl.ds(0, half), :] = part.astype(bf16)
                    out_ref[to, pl.ds(half, 16), :] = extra

    for ref, side in ((keep_ref, q), (give_ref, 1 - q)):
        ref[:, pl.ds(0, width)] = nat_ref[side, :, pl.ds(0, width)]
        rows_out = nat_ref[side, :, pl.ds(width, width)].astype(f32)
        ref[:, pl.ds(width, width)] = (weight * rows_out).astype(bf16)
        ref[:, pl.ds(2 * width, hidden)] = activation
        ref[:, pl.ds(2 * width + hidden, hidden)] = d_gate
        ref[:, pl.ds(2 * width + 2 * hidden, hidden)] = d_up


def prepare(base_ref, indices_ref, wg_ref, wu_ref, wd_ref, out_ref, pick_ref, wide_ref, sem):
    chunk = wg_ref.shape[1]
    pairs = [(wg_ref, out_ref.at[0]), (wu_ref, out_ref.at[1])] + [
        (wd_ref.at[:, pl.ds(i * chunk, chunk)], out_ref.at[2, pl.ds(i * chunk, chunk)])
        for i in range(wd_ref.shape[1] // chunk)
    ]
    copies = [
        pltpu.make_async_copy(source, target, sem.at[i])
        for i, (source, target) in enumerate(pairs)
    ]
    for copy in copies:
        copy.start()
    f32 = jnp.float32
    experts, capacity = indices_ref.shape
    groups = experts // 2
    peer = pick_ref.shape[0] // experts
    base = base_ref[0]
    lane = lax.broadcasted_iota(jnp.int32, (groups, capacity), 1).astype(f32)
    for member in range(2):
        tokens = indices_ref[pl.ds(member, groups, stride=2), :]
        live = tokens >= 0
        before = jnp.where(live & (tokens < base), 1.0, 0.0)
        start = jnp.sum(before, axis=1, keepdims=True)
        shifted = jnp.where(live, tokens - base + 1, 0).astype(f32)
        for place in range(peer):
            at_place = jnp.where(lane == start + place, shifted, 0.0)
            chosen = jnp.sum(at_place, axis=1, keepdims=True) - 1.0
            rows = pl.ds(member * groups * peer + place, groups, stride=peer)
            wide_ref[rows, :] = jnp.where(lane == chosen, 1.0, 0.0)
    pick_ref[...] = wide_ref[...].astype(pick_ref.dtype)
    for copy in copies:
        copy.wait()


def local(x_tokens, cotangent, w_gate, w_up, w_down, combine, indices):
    bf16 = jnp.bfloat16
    f32 = jnp.float32
    groups = lax.axis_size("z")
    spread = lax.axis_size("x") * lax.axis_size("c")
    tok_dev, part = x_tokens.shape
    experts, capacity = indices.shape
    exp_dev = experts // groups
    peer = 2 * capacity // groups
    z = lax.axis_index("z")
    p = lax.axis_index("p")
    q = lax.axis_index("q")
    wg = w_gate[0]
    wu = w_up[0]
    wd = w_down[0]

    table = jnp.concatenate([x_tokens, cotangent], axis=1)
    table = lax.ppermute(table, ("p", "q"), [(0, 0), (1, 2), (2, 1), (3, 3)])

    swap = [(0, 1), (1, 0)]
    here = pl.BlockSpec(memory_space=pltpu.HBM)
    whole = pl.BlockSpec(memory_space=pltpu.VMEM)
    packed, pick = pl.pallas_call(
        prepare,
        out_shape=(
            jax.ShapeDtypeStruct((3,) + wg.shape, bf16),
            jax.ShapeDtypeStruct((experts * peer, tok_dev), bf16),
        ),
        in_specs=[pl.BlockSpec(memory_space=pltpu.SMEM), whole] + [here] * 3,
        out_specs=(whole, whole),
        scratch_shapes=[
            pltpu.VMEM((experts * peer, tok_dev), f32),
            pltpu.SemaphoreType.DMA((6,)),
        ],
        cost_estimate=pl.CostEstimate(flops=0, bytes_accessed=3 << 20, transcendentals=0),
    )((z * tok_dev).reshape(1), indices, wg, wu, wd)
    packed, table = lax.optimization_barrier((packed, table))
    far = lax.ppermute(packed, "q", swap)

    slots = jnp.arange(capacity, dtype=jnp.int32)
    send = jnp.dot(pick, table, preferred_element_type=f32).astype(bf16)
    recv = lax.all_to_all(
        send.reshape(experts, peer, 2 * part), ("p", "z"), split_axis=0, concat_axis=0, tiled=True
    )

    own = lax.dynamic_slice_in_dim(indices, z * exp_dev, exp_dev, 0)
    cells = jnp.arange(groups * peer, dtype=jnp.int32)
    cell_block = cells // peer
    earlier = (own[:, None, :] >= 0) & (own[:, None, :] < cell_block[None, :, None] * tok_dev)
    own_want = jnp.sum(earlier.astype(jnp.int32), axis=2) + cells % peer
    own_block = jnp.where(own >= 0, own // tok_dev, -1)
    place = jnp.where(own_block[:, :, None] == cell_block[None, None, :], own_want[:, None, :], -1)
    place = (place == slots[None, :, None]).astype(bf16)
    own_place = lax.dynamic_index_in_dim(place, p, 0, keepdims=False)
    recv, far = lax.optimization_barrier((recv, far))
    recv = recv.reshape(2, groups * peer, 2 * part)
    taken = [jnp.dot(own_place, recv[i], preferred_element_type=f32).astype(bf16) for i in range(2)]
    compact = jnp.concatenate(
        [taken[0][:, :part], taken[1][:, :part], taken[0][:, part:], taken[1][:, part:]], axis=1
    )
    half_cap = capacity // 2
    compact = compact.reshape(2, 1, half_cap, 4 * part)
    spreadout = jnp.broadcast_to(compact, (2, spread, half_cap, 4 * part))
    gathered = lax.all_to_all(
        spreadout.reshape(2 * spread, half_cap, 4 * part),
        ("q", "x", "c"),
        split_axis=0,
        concat_axis=0,
        tiled=True,
    )
    hidden = wg.shape[1]
    width = wg.shape[0]
    weight = lax.dynamic_slice(combine, (p, q * half_cap), (1, half_cap)).reshape(half_cap, 1)
    vmem = pl.BlockSpec(memory_space=pltpu.VMEM)
    held = jax.ShapeDtypeStruct((half_cap, 2 * width + 3 * hidden), bf16)
    piece, keep, give = pl.pallas_call(
        middle,
        out_shape=(
            jax.ShapeDtypeStruct((4 * spread, half_cap // 2 + 16, 2 * part), bf16),
            held,
            held,
        ),
        in_specs=[pl.BlockSpec(memory_space=pltpu.SMEM)] + [vmem] * 2
        + [here] * 4,
        out_specs=(vmem, vmem, vmem),
        scratch_shapes=[
            pltpu.VMEM((2, half_cap, 2 * width), bf16),
            pltpu.VMEM((2,) + wg.shape, bf16),
            pltpu.VMEM((2,) + wu.shape, bf16),
            pltpu.VMEM((2,) + wd.shape, bf16),
            pltpu.SemaphoreType.DMA((5 + width // hidden,)),
        ],
        compiler_params=pltpu.CompilerParams(vmem_limit_bytes=52 * 1024 * 1024),
        cost_estimate=pl.CostEstimate(
            flops=20 * half_cap * width * hidden, bytes_accessed=5 << 20, transcendentals=0
        ),
    )(q.reshape(1), weight, gathered, wg, wu, wd, far)
    pieces = lax.all_to_all(piece, ("p", "q", "x", "c"), split_axis=0, concat_axis=0, tiled=True)
    pieces = pieces.reshape(2, 2, spread, half_cap // 2 + 16, 2 * part)
    summed = jnp.sum(pieces.astype(f32), axis=2)
    term_sum = summed[:, :, half_cap // 2]
    grad_combine = (term_sum[:, :, :half_cap] + term_sum[:, :, half_cap:]).reshape(
        exp_dev, capacity
    )
    summed = summed[:, :, : half_cap // 2].astype(bf16)
    summed = jnp.transpose(
        summed.reshape(exp_dev, 2, half_cap // 2, 2, part), (0, 1, 3, 2, 4)
    ).reshape(exp_dev, capacity, part)

    over_slots = (((0,), (0,)), ((), ()))
    back = jnp.concatenate(
        [
            lax.dot_general(place[i], summed[i], over_slots, preferred_element_type=f32).astype(bf16)
            for i in range(exp_dev)
        ],
        axis=1,
    )
    returned = lax.all_to_all(
        back.reshape(groups, peer, exp_dev * part), "z", split_axis=0, concat_axis=0, tiled=True
    ).reshape(groups * peer, exp_dev * part)
    pick = pick.reshape(exp_dev, groups * peer, tok_dev)
    grad_tokens = lax.dot_general(
        pick[0], returned[:, :part], over_slots, preferred_element_type=f32
    )
    grad_tokens = grad_tokens + lax.dot_general(
        pick[1], returned[:, part:], over_slots, preferred_element_type=f32
    )

    give, _ = lax.optimization_barrier((give, back))
    got = lax.all_gather(give, "q", axis=0)
    got = lax.dynamic_index_in_dim(got, 1 - q, 0, keepdims=False)
    both = jnp.concatenate([keep, got], axis=0)
    rows_in = both[:, :width]
    scaled_out = both[:, width : 2 * width]
    activation = both[:, 2 * width : 2 * width + hidden]
    d_gate = both[:, 2 * width + hidden : 2 * width + 2 * hidden]
    d_up = both[:, 2 * width + 2 * hidden :]
    grad_down = lax.dot_general(activation, scaled_out, over_slots, preferred_element_type=f32)
    grad_gate = lax.dot_general(rows_in, d_gate, over_slots, preferred_element_type=f32)
    grad_up = lax.dot_general(rows_in, d_up, over_slots, preferred_element_type=f32)
    return (
        grad_tokens.astype(bf16),
        grad_gate.astype(bf16)[None],
        grad_up.astype(bf16)[None],
        grad_down.astype(bf16)[None],
        grad_combine,
    )


def solution(mesh):
    groups, lanes = mesh.devices.shape
    split = Mesh(
        mesh.devices.reshape(groups, 2, 2, lanes // 8, 2), ("z", "p", "q", "x", "c")
    )
    mp = ("p", "q", "x", "c")
    placed = (
        P("z", mp),
        P("z", mp),
        P("z", None, mp),
        P("z", None, mp),
        P("z", mp, None),
        P("z", None),
        P(),
    )
    return jax.shard_map(
        local,
        mesh=split,
        in_specs=placed,
        out_specs=(
            P("z", mp),
            P("z", None, mp),
            P("z", None, mp),
            P("z", mp, None),
            P("z", None),
        ),
        check_vma=False,
    )
```
